256 devices in a mesh: gx: 16 (over z, x_lo), gz: 16 (over x_hi, y, core).
Axes of the slice: x: 4 (x_hi: 2, x_lo: 2; x = x_hi * 2 + x_lo), y: 4, z: 8, core: 2. Of those that a mesh axis runs over, the one named last changes fastest.
Arguments:
- moments: float32 [6, 2, 1024, 2048], P(None, None, 'gx', 'gz'), may hold values from 0.5 to 2
- scalars: float32 [12, 2, 1024, 2048], P(None, None, 'gx', 'gz'), may hold values from -4 to 4
- velocity: float32 [2, 2, 1024, 2048], P(None, None, 'gx', 'gz'), may hold values from -4 to 4
- diffusivity: float32 [18], replicated, may hold values from 0.05 to 0.5
- nucleation: float32 [2, 1024, 2048], P(None, 'gx', 'gz'), may hold values from 0.2 to 2
- growth: float32 [2, 1024, 2048], P(None, 'gx', 'gz'), may hold values from 0.1 to 1
Outputs:
- new_moments: float32 [6, 2, 1024, 2048], P(None, None, 'gx', 'gz')
- new_scalars: float32 [12, 2, 1024, 2048], P(None, None, 'gx', 'gz')
The draws below stay inside these ranges and needn't reach their ends.
All inputs are finite; a program needn't handle non-finite values.
Results may differ from the reference program's by a relative error of at most 0.00002.
Values sent between devices are 32-bit elements; how exact they have to be, the bound alone decides.
No kernel may reach another device: no remote copies, remote signals or barrier semaphores. Data moves between devices by JAX's collectives and lax.ppermute only.
A program may use at most 64 MiB of HBM per device.

```python
import math
import jax
import jax.numpy as jnp
from jax import lax

MOMENTS = 6
SCALARS = 12
NY = 2
NX = 1024
NZ = 2048


def levels(stream_key, extent, cuts, smallest, high):
    level, own = 1.0, jax.random.fold_in(stream_key, 6)
    for dim, blocks in cuts:
        steps = jnp.exp(jax.random.uniform(jax.random.fold_in(own, dim), (blocks,), jnp.float32, smallest / len(cuts), high / len(cuts)))
        level = level * jnp.repeat(steps, extent[dim] // blocks).reshape([-1 if axis == dim else 1 for axis in range(len(extent))])
    return level


def centred(stream_key, dims, width, most, cuts=(), kind=jnp.bfloat16):
    values = jax.random.normal(stream_key, dims, jnp.float32) * width
    if len(cuts) > 0:
        values = levels(stream_key, dims, cuts, -0.22, 0.18) * values
    return jnp.clip(values, min=-most, max=most).astype(kind)


def setup_inputs(seed: int = 0) -> dict:
    streams_of = jax.random.split(jax.random.key(seed), 7)
    return {
        "moments": jnp.clip(0.5 + 1.5 * jax.random.uniform(streams_of[0], (MOMENTS, NY, NX, NZ), jnp.float32) ** levels(streams_of[0], (MOMENTS, NY, NX, NZ), ((2, 16), (3, 16)), -0.2, 0.2), 0.5, 2.0),
        "scalars": centred(streams_of[1], (SCALARS, NY, NX, NZ), 1.0, 4.0, ((2, 16), (3, 16)), jnp.float32),
        "velocity": centred(streams_of[2], (2, NY, NX, NZ), 1.5, 4.0, ((2, 16), (3, 16)), jnp.float32),
        "diffusivity": jnp.clip(jnp.exp(jax.random.uniform(streams_of[3], (MOMENTS + SCALARS,), jnp.float32, math.log(0.05), math.log(0.5))), 0.05, 0.5),
        "nucleation": jnp.clip(jnp.exp(math.log(2.0) - 2.3025851 * jax.random.uniform(streams_of[4], (NY, NX, NZ), jnp.float32) ** levels(streams_of[4], (NY, NX, NZ), ((1, 16), (2, 16)), -0.2, 0.2)), 0.2, 2.0),
        "growth": jnp.clip(jnp.exp(math.log(1.0) - 2.3025851 * jax.random.uniform(streams_of[5], (NY, NX, NZ), jnp.float32) ** levels(streams_of[5], (NY, NX, NZ), ((1, 16), (2, 16)), -0.2, 0.2)), 0.1, 1.0),
    }


first_coef = (0.8, -0.2, 4.0 / 105.0, -1.0 / 280.0)
second_coef = (1.6, -0.2, 8.0 / 315.0, -1.0 / 560.0)
centre_coef = -205.0 / 72.0
time_step = 0.25


def sources(state, nucl, grow):
    precursor = state[6]
    birth = nucl * precursor * precursor
    moms = state[:6]
    earlier = jnp.concatenate([jnp.zeros_like(moms[:1]), moms[:5]], axis=0)
    orders = (jnp.arange(6, dtype=jnp.int32).astype(jnp.float32) / 3.0).reshape((6,) + (1,) * (moms.ndim - 1))
    mom_src = 0.5 * birth + grow * orders * earlier - 0.3 * moms[0] * moms
    return jnp.concatenate([mom_src, (-0.2 * birth)[None], jnp.zeros_like(state[7:])], axis=0)


def row_rhs(state, vel, kappa, nucl, grow):
    flux_x = vel[0] * state
    flux_z = vel[1] * state
    conv = jnp.zeros_like(state)
    lap = 2.0 * centre_coef * state
    for m in range(1, 5):
        conv = conv + first_coef[m - 1] * (jnp.roll(flux_x, -m, 1) - jnp.roll(flux_x, m, 1))
        conv = conv + first_coef[m - 1] * (jnp.roll(flux_z, -m, 2) - jnp.roll(flux_z, m, 2))
        lap = lap + second_coef[m - 1] * (jnp.roll(state, -m, 1) + jnp.roll(state, m, 1) + jnp.roll(state, -m, 2) + jnp.roll(state, m, 2))
    return -conv + kappa[:, None, None] * lap + sources(state, nucl, grow)


def reference(moments, scalars, velocity, diffusivity, nucleation, growth):
    state = jnp.concatenate([moments, scalars], axis=0)

    def one_row(items):
        q0, vel, nucl, grow = items
        q1 = q0 + time_step * row_rhs(q0, vel, diffusivity, nucl, grow)
        return 0.5 * q0 + 0.5 * (q1 + time_step * row_rhs(q1, vel, diffusivity, nucl, grow))

    rows = lax.map(one_row, (jnp.moveaxis(state, 1, 0), jnp.moveaxis(velocity, 1, 0), nucleation, growth))
    result = jnp.moveaxis(rows, 0, 1)
    return result[:6], result[6:]
```

```python
import jax
import jax.numpy as jnp
from jax import lax
from jax.experimental import pallas as pl
from jax.experimental.pallas import tpu as pltpu
from jax.sharding import PartitionSpec as P

first_coef = (0.8, -0.2, 4.0 / 105.0, -1.0 / 280.0)
second_coef = (1.6, -0.2, 8.0 / 315.0, -1.0 / 560.0)
centre_coef = -205.0 / 72.0
time_step = 0.25

ROWS = 64
F32 = jnp.float32


def lanes(shape=(8, 128)):
    return lax.broadcasted_iota(jnp.int32, shape, len(shape) - 1)


def roll(x, by):
    by = by % 128
    return x if by == 0 else pltpu.roll(x, by, 1)


def plane_ref(refs, p, s):
    mom, sca, vel, nuc, gro = refs
    c, ny = s // 2, s % 2
    if p < 9:
        f = p + 9 * c
        return mom.at[f, ny] if f < 6 else sca.at[f - 6, ny]
    if p == 9:
        return vel.at[c, ny]
    return (nuc, gro)[c].at[ny]


def pack_z(mom, sca, vel, nuc, gro, zl, zr):
    refs = (mom, sca, vel, nuc, gro)
    block = lanes() // 8

    def row(r, _):
        at = pl.ds(pl.multiple_of(r * 8, 8), 8)
        for t in range(3):
            left = right = jnp.zeros((8, 128), F32)
            for j in range(4):
                p = 4 * t + j
                if p > 10:
                    continue
                for s in range(4):
                    b = 4 * s + j
                    tile = plane_ref(refs, p, s)[at, :]
                    left = jnp.where(block == b, roll(tile, 8 * b), left)
                    right = jnp.where(block == b, roll(tile, 8 * b + 8), right)
            zl[t, at, :] = left
            zr[t, at, :] = right
        return _

    lax.fori_loop(0, 8, row, 0)


def pack_x(mom, sca, vel, nuc, gro, up, down):
    for msg, lo, part in ((down, 0, 0), (up, 56, 60)):
        for f in range(18):
            src = mom.at[f] if f < 6 else sca.at[f - 6]
            for ny in range(2):
                msg[2 * f + ny] = src[ny, lo : lo + 8, :]
        for c in range(2):
            for ny in range(2):
                msg[36 + 2 * c + ny] = vel[c, ny, lo : lo + 8, :]
        for ny in range(2):
            msg[40 + ny, 0:4, :] = nuc[ny, part : part + 4, :]
            msg[40 + ny, 4:8, :] = gro[ny, part : part + 4, :]


def edge_packs(zl, zr, from_left, from_right, up_in, down_in, packs, up, down, buf, sems):
    del up_in, down_in
    sub = (lanes() // 8) % 4
    for p in range(11):
        t, j = p // 4, p % 4
        for r in range(0, 64, 8):
            e = roll(from_left[t, r : r + 8, :], -8 * j)
            e = jnp.where(sub == 1, roll(zl[t, r : r + 8, :], 8 - 8 * j), e)
            e = jnp.where(sub == 2, roll(zr[t, r : r + 8, :], 16 - 8 * j), e)
            e = jnp.where(sub == 3, roll(from_right[t, r : r + 8, :], 24 - 8 * j), e)
            packs[p, r : r + 8, :] = e
            if p < 10:
                at = slice(4 * (p % 2), 4 * (p % 2) + 4)
                if r == 0:
                    buf[0, p // 2, at, :] = e[0:4]
                if r == 56:
                    buf[1, p // 2, at, :] = e[4:8]
    copies = [
        pltpu.make_async_copy(buf.at[k], msg.at[pl.ds(42, 5)], sems.at[k])
        for k, msg in enumerate((down, up))
    ]
    for copy in copies:
        copy.start()
    for copy in copies:
        copy.wait()


def transport(q, g, q_at, f_at, kappa, scale):
    k = kappa * scale
    lap = (2.0 * centre_coef) * q
    conv = None
    acc = None
    for m in range(1, 5):
        a, b = first_coef[m - 1] * scale, second_coef[m - 1]
        lap = lap + b * (q_at(m) + q_at(-m))
        c = a * (f_at(-m) - f_at(m))
        conv = c if conv is None else conv + c
        kq = (k * b) * q
        ag = a * g
        z = roll(kq - ag, -m) + roll(kq + ag, m)
        acc = z if acc is None else acc + z
    return k * lap + conv + acc


def correction(q, g, kappa, scale):
    lane = lanes() % 32
    low = lane < 16
    outer = ((lane >= 4) & (lane < 8)) | ((lane >= 24) & (lane < 28))

    def gap(x):
        return jnp.where(outer, x - jnp.where(low, roll(x, -16), roll(x, 16)), 0.0)

    dq, dg = gap(q), gap(g)
    dg = jnp.where(low, dg, -dg)
    k = kappa * scale
    left = right = None
    for m in range(1, 5):
        both = (k * second_coef[m - 1]) * dq + (first_coef[m - 1] * scale) * dg
        one, two = roll(both, m + 16), roll(both, -m)
        left = one if left is None else left + one
        right = two if right is None else right + two
    return jnp.where(lane < 24, right, left)


def unpack(tile, s):
    lane = lanes()
    return jnp.where((lane < 4) | (lane >= 124), roll(tile, 104 - 32 * s), 0.0)


def sources(get, nucl, grow, scale):
    y = get(6)
    birth = nucl * y * y
    first = get(0)
    moms = [first] + [get(k) for k in range(1, 6)]
    half = (0.5 * scale) * birth
    sink = (0.3 * scale) * first
    out = []
    for k in range(6):
        s = half - sink * moms[k]
        if k:
            s = s + (scale * k / 3.0) * grow * moms[k - 1]
        out.append(s)
    return out + [(-0.2 * scale) * birth]


def pack_sources(get, ng, scale):
    low = lanes() < 64
    nucl = jnp.where(low, ng, 0.0)
    grow = jnp.where(low, roll(ng, 64), 0.0)
    y = get(6)
    birth = nucl * y * y
    moms = [get(k) for k in range(6)]
    sink = jnp.where(low, (0.3 * scale) * moms[0], 0.0)
    out = []
    for k in range(6):
        s = (0.5 * scale) * birth - sink * moms[k]
        if k:
            s = s + (scale * k / 3.0) * grow * moms[k - 1]
        out.append(s)
    return out + [(-0.2 * scale) * birth]


def pack_velocity(tile):
    low = lanes() < 64
    other = roll(tile, 64)
    return jnp.where(low, tile, other), jnp.where(low, other, tile)


def pack_kappa(kappa, p):
    return jnp.where(lanes() < 64, kappa[p], kappa[p + 9])


def ds(start, size):
    return slice(start, start + size)


def pack_stage(q, pu, pw, png, kappa, f, cor, dest, rows, base, scale):
    first, last = rows[0], rows[-1] + 8

    def one(p, _):
        kap = pack_kappa(kappa, p)
        lo, hi = max(first - 4, 0), last + 4
        for r in range(lo // 8 * 8, hi, 8):
            f[ds(r, 8), :] = pu[ds(r, 8), :] * q[p, ds(r, 8), :]
        for r in rows:
            v = q[p, ds(r, 8), :]
            g = pw[ds(r, 8), :] * v
            cor[p, ds(r - base, 8), :] = correction(v, g, kap, scale)
            rate = transport(
                v, g, lambda m: q[p, ds(r + m, 8), :], lambda m: f[ds(r + m, 8), :], kap, scale
            )
            dest[p, ds(r - base, 8), :] = v + rate
        return _

    lax.fori_loop(0, 9, one, 0)
    for r in rows:
        src = pack_sources(lambda k: q[k, ds(r, 8), :], png[ds(r, 8), :], scale)
        for k in range(7):
            dest[k, ds(r - base, 8), :] += src[k]


def planes(p):
    for slot in range(4):
        field, ny = p + 9 * (slot // 2), slot % 2
        yield 2 * field + ny, field, ny, slot


def interior(
    kappa, mom, sca, vel, nuc, gro, packs, out_mom, out_sca, edge, pack_edge,
    q, q1, f, pu, pw, pq1, cor, half,
):
    for k in range(18):
        src = mom.at[k] if k < 6 else sca.at[k - 6]
        for ny in range(2):
            q[2 * k + ny] = src[ny]
    for r in range(0, 64, 8):
        pu[ds(r, 8), :], pw[ds(r, 8), :] = pack_velocity(packs[9, ds(r, 8), :])
    dt = time_step

    rows = list(range(4, 60, 8))
    pack_stage(packs, pu, pw, packs.at[10], kappa, f, cor, pq1, rows, 4, dt)

    def one(p, _):
        for i, field, ny, slot in planes(p):
            kap = kappa[field]
            for r in range(0, 64, 8):
                f[ds(r, 8), :] = vel[0, ny, ds(r, 8), :] * q[i, ds(r, 8), :]
            for r in rows:
                v = q[i, ds(r, 8), :]
                g = vel[1, ny, ds(r, 8), :] * v
                rate = transport(
                    v, g, lambda m: q[i, ds(r + m, 8), :], lambda m: f[ds(r + m, 8), :], kap, dt
                )
                q1[i, ds(r - 4, 8), :] = v + rate + unpack(cor[p, ds(r - 4, 8), :], slot)
        return _

    lax.fori_loop(0, 9, one, 0)
    for ny in range(2):
        for r in rows:
            src = sources(
                lambda k: q[2 * k + ny, ds(r, 8), :],
                nuc[ny, ds(r, 8), :], gro[ny, ds(r, 8), :], dt,
            )
            for k in range(7):
                q1[2 * k + ny, ds(r - 4, 8), :] += src[k]
    for i in range(36):
        edge[0, i] = q1[i, 0:8, :]
        edge[1, i] = q1[i, 48:56, :]
    for p in range(9):
        pack_edge[0, p] = pq1[p, 0:8, :]
        pack_edge[1, p] = pq1[p, 48:56, :]

    scale = 0.5 * dt
    rows = list(range(8, 56, 8))

    def two(p, _):
        kap = pack_kappa(kappa, p)
        for r in rows:
            v = pq1[p, ds(r - 4, 8), :]
            cor[p, ds(r, 8), :] = correction(v, pw[ds(r, 8), :] * v, kap, scale)
        for i, field, ny, slot in planes(p):
            kap = kappa[field]
            for r in range(4, 60, 8):
                f[ds(r - 4, 8), :] = vel[0, ny, ds(r, 8), :] * q1[i, ds(r - 4, 8), :]
            for r in rows:
                v = q1[i, ds(r - 4, 8), :]
                g = vel[1, ny, ds(r, 8), :] * v
                rate = transport(
                    v, g, lambda m: q1[i, ds(r - 4 + m, 8), :], lambda m: f[ds(r - 4 + m, 8), :],
                    kap, scale,
                )
                add = unpack(cor[p, ds(r, 8), :], slot)
                half[i, ds(r, 8), :] = 0.5 * (q[i, ds(r, 8), :] + v) + rate + add
        return _

    lax.fori_loop(0, 9, two, 0)
    for ny in range(2):
        for r in rows:
            src = sources(
                lambda k: q1[2 * k + ny, ds(r - 4, 8), :],
                nuc[ny, ds(r, 8), :], gro[ny, ds(r, 8), :], scale,
            )
            for k in range(7):
                half[2 * k + ny, ds(r, 8), :] += src[k]
    for k in range(18):
        dst = out_mom.at[k] if k < 6 else out_sca.at[k - 6]
        for ny in range(2):
            dst[ny, 8:56, :] = half[2 * k + ny, 8:56, :]


def edges(
    kappa, mom, sca, vel, nuc, gro, packs, edge, pack_edge, above, below, in_mom, in_sca, out_mom, out_sca,
    q, q1, f, vq, v1, ng, pq, pu, pw, png, pq1, cor, half,
):
    del in_mom, in_sca
    step = pl.program_id(0)
    own8 = pl.ds(pl.multiple_of(8 * (1 - step), 8), 8)
    far8 = pl.ds(pl.multiple_of(8 * step, 8), 8)
    mid = slice(4, 12)
    dt = time_step

    def take(msg):
        for i in range(36):
            q[i, far8, :] = msg[i]
        for i in range(4):
            vq[i, far8, :] = msg[36 + i]
        for ny in range(2):
            ng[ny, mid, :] = nuc[ny]
            ng[2 + ny, mid, :] = gro[ny]

    @pl.when(step == 0)
    def _():
        take(above)
        for ny in range(2):
            ng[ny, 0:4, :] = above[40 + ny, 0:4, :]
            ng[2 + ny, 0:4, :] = above[40 + ny, 4:8, :]
        for c in range(2):
            for ny in range(2):
                v1[2 * c + ny, 0:4, :] = above[36 + 2 * c + ny, 4:8, :]
                v1[2 * c + ny, 4:16, :] = vel[c, ny, 0:12, :]
        for p in range(10):
            pq[p, 0:4, :] = jnp.zeros((4, 128), F32)
            pq[p, 4:8, :] = above[42 + p // 2, ds(4 * (p % 2), 4), :]

    @pl.when(step == 1)
    def _():
        take(below)
        for ny in range(2):
            ng[ny, 12:16, :] = below[40 + ny, 0:4, :]
            ng[2 + ny, 12:16, :] = below[40 + ny, 4:8, :]
        for c in range(2):
            for ny in range(2):
                v1[2 * c + ny, 0:12, :] = vel[c, ny, 52:64, :]
                v1[2 * c + ny, 12:16, :] = below[36 + 2 * c + ny, 0:4, :]
        for p in range(10):
            pq[p, 8:12, :] = below[42 + p // 2, ds(4 * (p % 2), 4), :]
            pq[p, 12:16, :] = jnp.zeros((4, 128), F32)

    own_at = pl.ds(pl.multiple_of(56 * step, 8), 8)
    for k in range(18):
        src = mom.at[k] if k < 6 else sca.at[k - 6]
        for ny in range(2):
            q[2 * k + ny, own8, :] = src[ny]
            q1[2 * k + ny, own8, :] = edge[0, 2 * k + ny]
    for c in range(2):
        for ny in range(2):
            vq[2 * c + ny, own8, :] = vel[c, ny, own_at, :]
    for p in range(10):
        pq[p, own8, :] = packs[p]
    for p in range(9):
        pq1[p, own8, :] = pack_edge[0, p]
    png[far8, :] = jnp.zeros((8, 128), F32)
    png[own8, :] = packs[10]
    for r in (0, 8):
        pu[ds(r, 8), :], pw[ds(r, 8), :] = pack_velocity(pq[9, ds(r, 8), :])

    def one(p, _):
        kap = pack_kappa(kappa, p)
        for r in (0, 8):
            f[4, ds(r, 8), :] = pu[ds(r, 8), :] * pq[p, ds(r, 8), :]
        v = pq[p, mid, :]
        g = pw[mid, :] * v
        cor = correction(v, g, kap, dt)
        pq1[p, far8, :] = v + transport(
            v, g, lambda m: pq[p, ds(4 + m, 8), :], lambda m: f[4, ds(4 + m, 8), :], kap, dt
        )
        for i, field, ny, slot in planes(p):
            for r in (0, 8):
                f[slot, ds(r, 8), :] = vq[ny, ds(r, 8), :] * q[i, ds(r, 8), :]
            v = q[i, mid, :]
            g = vq[2 + ny, mid, :] * v
            rate = transport(
                v, g, lambda m: q[i, ds(4 + m, 8), :], lambda m: f[slot, ds(4 + m, 8), :],
                kappa[field], dt,
            )
            q1[i, far8, :] = v + rate + unpack(cor, slot)
        return _

    lax.fori_loop(0, 9, one, 0)
    src = pack_sources(lambda k: pq[k, mid, :], png[mid, :], dt)
    for k in range(7):
        pq1[k, far8, :] += src[k]
    for ny in range(2):
        src = sources(lambda k: q[2 * k + ny, mid, :], ng[ny, far8, :], ng[2 + ny, far8, :], dt)
        for k in range(7):
            q1[2 * k + ny, far8, :] += src[k]

    scale = 0.5 * dt

    def two(p, _):
        v = pq1[p, mid, :]
        cor = correction(v, pw[own8, :] * v, pack_kappa(kappa, p), scale)
        for i, field, ny, slot in planes(p):
            for r in (0, 8):
                f[slot, ds(r, 8), :] = v1[ny, ds(r, 8), :] * q1[i, ds(r, 8), :]
            v = q1[i, mid, :]
            g = v1[2 + ny, mid, :] * v
            rate = transport(
                v, g, lambda m: q1[i, ds(4 + m, 8), :], lambda m: f[slot, ds(4 + m, 8), :],
                kappa[field], scale,
            )
            half[i] = 0.5 * (q[i, own8, :] + v) + rate + unpack(cor, slot)
        return _

    lax.fori_loop(0, 9, two, 0)
    for ny in range(2):
        src = sources(lambda k: q1[2 * k + ny, mid, :], ng[ny, mid, :], ng[2 + ny, mid, :], scale)
        for k in range(7):
            half[2 * k + ny] += src[k]
    for k in range(18):
        dst = out_mom.at[k] if k < 6 else out_sca.at[k - 6]
        for ny in range(2):
            dst[ny] = half[2 * k + ny]


def call(kernel, outs, cost, **kw):
    return pl.pallas_call(
        kernel,
        out_shape=[jax.ShapeDtypeStruct(o, F32) for o in outs],
        cost_estimate=pl.CostEstimate(flops=cost, bytes_accessed=cost // 4, transcendentals=0),
        compiler_params=pltpu.CompilerParams(vmem_limit_bytes=24 * 2**20),
        **kw,
    )


def send(value, axis, by):
    peers = lax.axis_size(axis)
    return lax.ppermute(value, axis, [(i, (i + by) % peers) for i in range(peers)])


def body(moments, scalars, velocity, diffusivity, nucleation, growth):
    fields = (moments, scalars, velocity, nucleation, growth)
    vmem = pl.BlockSpec(memory_space=pltpu.VMEM)
    smem = pl.BlockSpec(memory_space=pltpu.SMEM)
    hbm = pl.BlockSpec(memory_space=pl.ANY)
    tiles = lambda *lead: pltpu.VMEM(lead + (128,), F32)

    zl, zr = call(pack_z, [(3, 64, 128)] * 2, 10**6)(*fields)
    from_right = send(zl, "gz", -1)
    from_left = send(zr, "gz", 1)
    up, down = call(pack_x, [(47, 8, 128)] * 2, 10**6)(*fields)
    packs, up, down = call(
        edge_packs,
        [(11, 64, 128), (47, 8, 128), (47, 8, 128)],
        10**6,
        in_specs=[vmem] * 4 + [hbm] * 2,
        out_specs=[vmem, hbm, hbm],
        input_output_aliases={4: 1, 5: 2},
        scratch_shapes=[tiles(2, 5, 8), pltpu.SemaphoreType.DMA((2,))],
    )(zl, zr, from_left, from_right, up, down)
    above = send(up, "gx", 1)
    below = send(down, "gx", -1)
    out_mom, out_sca, edge, pack_edge = call(
        interior,
        [moments.shape, scalars.shape, (2, 36, 8, 128), (2, 9, 8, 128)],
        10**8,
        in_specs=[smem] + [vmem] * 6,
        scratch_shapes=[
            tiles(36, 64), tiles(36, 56), tiles(64), tiles(64), tiles(64), tiles(9, 56), tiles(9, 64), tiles(36, 64),
        ],
    )(diffusivity, *fields, packs)

    def row_block(*lead):
        return pl.BlockSpec(lead + (8, 128), lambda i: (0,) * len(lead) + (7 * i, 0))

    def side_block(*lead):
        return pl.BlockSpec((1,) + lead + (8, 128), lambda i: (i,) + (0,) * (len(lead) + 2))

    def whole(*shape):
        return pl.BlockSpec(shape, lambda i: (0,) * len(shape))

    return tuple(
        call(
            edges,
            [moments.shape, scalars.shape],
            10**8,
            grid=(2,),
            in_specs=[
                smem, row_block(6, 2), row_block(12, 2), whole(2, 2, 64, 128), row_block(2), row_block(2), row_block(11),
                side_block(36), side_block(9), whole(47, 8, 128), whole(47, 8, 128), hbm, hbm,
            ],
            out_specs=[row_block(6, 2), row_block(12, 2)],
            input_output_aliases={11: 0, 12: 1},
            scratch_shapes=[
                tiles(36, 16), tiles(36, 16), tiles(5, 16), tiles(4, 16), tiles(4, 16), tiles(4, 16), tiles(10, 16),
                tiles(16), tiles(16), tiles(16), tiles(9, 16), tiles(8), tiles(36, 8),
            ],
        )(diffusivity, *fields, packs, edge, pack_edge, above, below, out_mom, out_sca)
    )


def solution(mesh):
    return jax.shard_map(
        body,
        mesh=mesh,
        in_specs=(
            P(None, None, "gx", "gz"),
            P(None, None, "gx", "gz"),
            P(None, None, "gx", "gz"),
            P(),
            P(None, "gx", "gz"),
            P(None, "gx", "gz"),
        ),
        out_specs=(P(None, None, "gx", "gz"), P(None, None, "gx", "gz")),
        check_vma=False,
    )
```

```python
import numpy as np

import jax
import jax.numpy as jnp
from jax import lax
from jax.experimental import pallas as pl
from jax.experimental.pallas import tpu as pltpu
from jax.sharding import PartitionSpec as P

first_whole, first_part = (672.0, -168.0, 32.0, -3.0), 840.0
second_whole, second_part = (8064.0, -1008.0, 128.0, -9.0), 5040.0
centre_x, centre_z = -28672.0, -28.0
time_step = 0.25

F32, BF16 = jnp.float32, jnp.bfloat16


def band(targets, sources, centre):
    gap = np.asarray(sources)[None, :] - np.asarray(targets)[:, None]
    second = np.where(gap == 0, centre, 0.0)
    first = np.zeros(gap.shape)
    for m in range(1, 5):
        second = second + second_whole[m - 1] * (abs(gap) == m)
        first = first - first_whole[m - 1] * ((gap == m) * 1.0 - (gap == -m))
    return second, first


def matrices():
    both = lambda pair, axis: np.concatenate([pair[0], pair[0], pair[1], pair[1]], axis=axis).astype(BF16)
    rows, cols = np.arange(64), np.arange(128)
    a_rows = both(band(rows, rows, centre_x), 1)
    place, away = np.arange(32), 1000
    part = np.concatenate([place[:16], away + place[16:]])
    a_edge = both(band(np.concatenate([part[4:12], part[20:28]]), part, centre_x), 1)
    z_main = both(tuple(m.T for m in band(cols, cols, centre_z)), 0)
    slot_col = np.concatenate([np.arange(-8, 8), np.arange(120, 136)])
    beyond = (slot_col < 0) | (slot_col >= 128)
    to_planes = []
    for matrix in band(cols, slot_col, 0.0):
        wide = np.zeros((128, 512))
        for s in range(4):
            wide[32 * s : 32 * s + 32, 128 * s : 128 * s + 128] = (matrix * beyond[None, :]).T
        to_planes.append(wide)
    lane = np.arange(128)
    in_slot = [m.T * (lane[:, None] // 16 == lane[None, :] // 16) for m in band(lane, lane, centre_z)]
    z_pack = both(tuple(np.concatenate([w, o], axis=1) for w, o in zip(to_planes, in_slot)), 0)
    return a_rows, a_edge, z_main, z_pack


def lanes(shape=(8, 128)):
    return lax.broadcasted_iota(jnp.int32, shape, len(shape) - 1)


def roll(x, by):
    by = by % 128
    return x if by == 0 else pltpu.roll(x, by, 1)


def split(x):
    high = x.astype(BF16)
    return high, (x - high.astype(F32)).astype(BF16)


def dot(a, b):
    return jnp.dot(a, b, preferred_element_type=F32)


def plane_of(p, s):
    c, ny = s // 2, s % 2
    return 2 * (p + 9 * c) + ny if p < 9 else 4 * p + s


def pack_z(mom, sca, vel, nuc, gro, zl, zr, fields, sems):
    parts = [
        [(mom, 0, 0, 8), (sca, 6, 18, 8)],
        [(mom, 8, 8, 4), (sca, 0, 12, 4), (sca, 14, 26, 8)],
        [(sca, 4, 16, 2), (sca, 22, 34, 2), (vel, 0, 36, 4), (nuc, 0, 40, 2), (gro, 0, 42, 2)],
    ]
    copies, n = [], 0
    for part in parts:
        copies.append([])
        for src, at, to, size in part:
            copies[-1].append(
                pltpu.make_async_copy(src.at[pl.ds(at, size)], fields.at[pl.ds(to, size)], sems.at[n])
            )
            copies[-1][-1].start()
            n += 1
    pair, odd = lanes() // 16, (lanes() // 8) % 2 == 1
    for t in range(3):
        for copy in copies[t]:
            copy.wait()
        for r in range(0, 64, 8):
            tile = [None, None]
            for j in range(4 if t < 2 else 3):
                for s in range(4):
                    c = 2 * s + j // 2
                    one = roll(fields[plane_of(4 * t + j, s), r : r + 8, :], 16 * c + 8)
                    half = tile[j % 2]
                    tile[j % 2] = one if half is None else jnp.where(pair == c, one, half)
            zr[t, r : r + 8, :] = jnp.where(odd, roll(tile[1], 8), tile[0])
            zl[t, r : r + 8, :] = jnp.where(odd, tile[1], roll(tile[0], -8))


def prepare(mom, sca, vel, nuc, gro, fields, own, up, down):
    for src, to in ((mom, 0), (sca, 12), (vel, 36), (nuc, 40), (gro, 42)):
        for k in range(src.shape[0]):
            fields[to + k] = src[k]
    for msg, lo, part in ((down, 0, 0), (up, 56, 60)):
        for i in range(38):
            msg[i] = fields[i, lo : lo + 8, :]
        for k in range(3):
            for side in range(2):
                i = 38 + side if k == 0 else 39 + k + 2 * side
                msg[38 + k, 4 * side : 4 * side + 4, :] = fields[i, part : part + 4, :]
    sub = lanes() // 8
    for p in range(11):
        for r in range(0, 64, 8):
            e = jnp.zeros((8, 128), F32)
            for s in range(4):
                tile = fields[plane_of(p, s), r : r + 8, :]
                e = jnp.where(sub == 4 * s + 1, roll(tile, 32 * s + 8), e)
                e = jnp.where(sub == 4 * s + 2, roll(tile, 32 * s + 24), e)
            own[p, r : r + 8, :] = e


def corners(from_left, from_right, up_in, down_in, up, down, buf, sems):
    del up_in, down_in
    first = lanes((4, 128)) % 8 < 4
    for k, part in enumerate((0, 60)):
        for t in range(3):
            at = slice(4 * (t % 2), 4 * (t % 2) + 4)
            rows = slice(part, part + 4)
            buf[k, t // 2, at, :] = jnp.where(first, from_right[t, rows, :], from_left[t, rows, :])
        buf[k, 1, 4:8, :] = jnp.zeros((4, 128), F32)
    copies = [
        pltpu.make_async_copy(buf.at[k], msg.at[pl.ds(41, 2)], sems.at[k])
        for k, msg in enumerate((down, up))
    ]
    for copy in copies:
        copy.start()
    for copy in copies:
        copy.wait()


def fill_packs(own, from_left, from_right, packs):
    sub = (lanes((64, 128)) // 8) % 4
    for p in range(11):
        t, j = p // 4, p % 4
        e = jnp.where(sub == 0, roll(from_left[t], -8 * j), own[p])
        packs[p] = jnp.where(sub == 3, roll(from_right[t], 24 - 8 * j), e)


def sources(get, nucl, grow, scale):
    y = get(6)
    birth = nucl * y * y
    moms = [get(k) for k in range(6)]
    half = (0.5 * scale) * birth
    sink = (0.3 * scale) * moms[0]
    out = []
    for k in range(6):
        s = half - sink * moms[k]
        if k:
            s = s + ((scale * k / 3.0) * grow) * moms[k - 1]
        out.append(s)
    return out + [(-0.2 * scale) * birth]


def pack_sources(get, ng, scale):
    low = lanes(ng.shape) < 64
    nucl = jnp.where(low, ng, 0.0)
    grow = jnp.where(low, roll(ng, 64), 0.0)
    y = get(6)
    birth = nucl * y * y
    moms = [get(k) for k in range(6)]
    half = (0.5 * scale) * birth
    sink = jnp.where(low, (0.3 * scale) * moms[0], 0.0)
    out = []
    for k in range(6):
        s = half - sink * moms[k]
        if k:
            s = s + ((scale * k / 3.0) * grow) * moms[k - 1]
        out.append(s)
    return out + [(-0.2 * scale) * birth]


def pack_velocity(tile):
    low = lanes(tile.shape) < 64
    other = roll(tile, 64)
    return jnp.where(low, tile, other), jnp.where(low, other, tile)


def pack_kappa(kappa, p):
    return jnp.where(lanes((1, 128)) < 64, kappa[p], kappa[p + 9])


def planes(p):
    for slot in range(4):
        field, ny = p + 9 * (slot // 2), slot % 2
        yield 2 * field + ny, field, ny, slot


def across(kq, g):
    return jnp.concatenate([*split(kq), *split(g)], axis=1)


def down_rows(kq, f):
    return jnp.concatenate([*split(kq), *split(f)], axis=0)


GROUP = 3


def interior(
    kappa, fields, own, from_left, from_right, a_rows, z_main, z_pack, packs, q1, pq1, half,
    us, ws, pus, pws, el, eo,
):
    def velocities(scale):
        for ny in range(2):
            us[ny] = fields[36 + ny] * (scale / first_part)
            ws[ny] = fields[38 + ny] * (scale / first_part)
        pu, pw = pack_velocity(packs[9])
        pus[...] = pu * (scale / first_part)
        pws[...] = pw * (scale / first_part)

    fill_packs(own, from_left, from_right, packs)
    dt = time_step
    velocities(dt)
    for p in range(9):
        e = packs[p]
        kq = (pack_kappa(kappa, p) * (dt / second_part)) * e
        el[64 * p : 64 * p + 64, :] = across(kq, pws[...] * e)
    eo[...] = dot(el[...], z_pack[...])
    for p in range(9):
        e = packs[p]
        kq = (pack_kappa(kappa, p) * (dt / second_part)) * e
        x = dot(a_rows[...], down_rows(kq, pus[...] * e))
        pq1[p] = e + x + eo[64 * p : 64 * p + 64, 512:640]
    src = pack_sources(lambda k: packs[k], packs[10], dt)
    for k in range(7):
        pq1[k] += src[k]

    def one(p):
        lhs, rhs = [], []
        for i, field, ny, slot in planes(p):
            v = fields[i]
            kq = (kappa[field] * (dt / second_part)) * v
            lhs.append(across(kq, ws[ny] * v))
            rhs.append(down_rows(kq, us[ny] * v))
        z = dot(jnp.concatenate(lhs, axis=0), z_main[...])
        x = [dot(a_rows[...], jnp.concatenate(rhs[c : c + 2], axis=1)) for c in (0, 2)]
        for i, field, ny, slot in planes(p):
            q1[i] = (
                fields[i]
                + z[64 * slot : 64 * slot + 64]
                + x[slot // 2][:, 128 * ny : 128 * ny + 128]
                + eo[pl.ds(64 * p, 64), 128 * slot : 128 * slot + 128]
            )

    def groups(fn):
        def step(i, _):
            for k in range(GROUP):
                fn(i * GROUP + k)
            return _

        if GROUP == 9:
            for p in range(9):
                fn(p)
        else:
            lax.fori_loop(0, 9 // GROUP, step, 0)

    groups(one)
    for ny in range(2):
        src = sources(lambda k: fields[2 * k + ny], fields[40 + ny], fields[42 + ny], dt)
        for k in range(7):
            q1[2 * k + ny] += src[k]

    scale = 0.5 * dt
    velocities(scale)
    for p in range(9):
        e = pq1[p, 8:56, :]
        kq = (pack_kappa(kappa, p) * (scale / second_part)) * e
        el[48 * p : 48 * p + 48, :] = across(kq, pws[8:56, :] * e)
    eo[0:432, 0:512] = dot(el[0:432, :], z_pack[:, 0:512])

    def two(p):
        lhs, rhs = [], []
        for i, field, ny, slot in planes(p):
            v = q1[i]
            kq = (kappa[field] * (scale / second_part)) * v
            mid = v[8:56]
            lhs.append(across(kq[8:56], ws[ny, 8:56, :] * mid))
            rhs.append(down_rows(kq, us[ny] * v))
        z = dot(jnp.concatenate(lhs, axis=0), z_main[...])
        x = [dot(a_rows[8:56, :], jnp.concatenate(rhs[c : c + 2], axis=1)) for c in (0, 2)]
        for i, field, ny, slot in planes(p):
            half[i, 8:56, :] = (
                0.5 * (fields[i, 8:56, :] + q1[i, 8:56, :])
                + z[48 * slot : 48 * slot + 48]
                + x[slot // 2][:, 128 * ny : 128 * ny + 128]
                + eo[pl.ds(48 * p, 48), 128 * slot : 128 * slot + 128]
            )

    groups(two)
    for ny in range(2):
        src = sources(
            lambda k: q1[2 * k + ny, 8:56, :], fields[40 + ny, 8:56, :], fields[42 + ny, 8:56, :], scale
        )
        for k in range(7):
            half[2 * k + ny, 8:56, :] += src[k]


def edges(
    kappa, fields, packs, q1, pq1, half, above, below, a_edge, z_main, z_pack, out_mom, out_sca,
    q, s1, vq, v1, pq, ps1, pvq, el, eo, done, sems,
):
    outs = [(out_mom, 0, 12), (out_sca, 12, 24)]
    copies = [
        pltpu.make_async_copy(
            half.at[pl.ds(at, size), pl.ds(8, 48)], out.at[pl.ds(0, size), pl.ds(8, 48)], sems.at[n]
        )
        for n, (out, at, size) in enumerate(outs)
    ]
    for copy in copies:
        copy.start()
    dt = time_step
    top, low = slice(4, 12), slice(20, 28)
    mid = lambda ref, *at: jnp.concatenate([ref[*at, top, :], ref[*at, low, :]], axis=0)

    for i in range(36):
        q[i, 0:8, :] = above[i]
        q[i, 8:16, :] = fields[i, 0:8, :]
        q[i, 16:24, :] = fields[i, 56:64, :]
        q[i, 24:32, :] = below[i]
        s1[i, 8:16, :] = q1[i, 4:12, :]
        s1[i, 16:24, :] = q1[i, 52:60, :]
    one, two = dt / first_part, 0.5 * dt / first_part
    for i in range(4):
        k = 36 + i
        if i < 2:
            vq[i, 0:8, :] = above[k] * one
            vq[i, 24:32, :] = below[k] * one
        else:
            at = slice(4 * (i % 2), 4 * (i % 2) + 4)
            vq[i, 0:4, :] = vq[i, 28:32, :] = jnp.zeros((4, 128), F32)
            vq[i, 4:8, :] = above[38, at, :] * one
            vq[i, 24:28, :] = below[38, at, :] * one
        vq[i, 8:16, :] = fields[k, 0:8, :] * one
        vq[i, 16:24, :] = fields[k, 56:64, :] * one
        v1[i, 0:4, :] = vq[i, 4:8, :] * 0.5
        v1[i, 4:16, :] = fields[k, 0:12, :] * two
        v1[i, 16:28, :] = fields[k, 52:64, :] * two
        v1[i, 28:32, :] = vq[i, 24:28, :] * 0.5
    zeros = jnp.zeros((4, 128), F32)
    lane = lanes() % 32
    is_left, is_right = (lane >= 4) & (lane < 8), (lane >= 24) & (lane < 28)
    for p in range(10):
        t, j = p // 4, p % 4
        at = slice(4 * (t % 2), 4 * (t % 2) + 4)
        corner = jnp.concatenate([above[41 + t // 2, at, :], below[41 + t // 2, at, :]], axis=0)
        corner = jnp.where(
            is_left, roll(corner, -8 * j), jnp.where(is_right, roll(corner, 24 - 8 * j), 0.0)
        )
        pq[p, 0:4, :] = zeros
        pq[p, 4:8, :] = corner[0:4]
        pq[p, 8:16, :] = packs[p, 0:8, :]
        pq[p, 16:24, :] = packs[p, 56:64, :]
        pq[p, 24:28, :] = corner[4:8]
        pq[p, 28:32, :] = zeros
    for p in range(9):
        ps1[p, 8:16, :] = pq1[p, 4:12, :]
        ps1[p, 16:24, :] = pq1[p, 52:60, :]
    pu, pw = pack_velocity(pq[9])
    pvq[0], pvq[1] = pu * one, pw * one

    def stage(src, vel, scale, put):
        def one(p):
            lhs, rhs = [], []
            for i, field, ny, slot in planes(p):
                k = kappa[field] * (scale / second_part)
                v, m = src[i], mid(src, i)
                lhs.append(across(k * m, mid(vel, 2 + ny) * m))
                rhs.append(down_rows(k * v, vel[ny] * v))
            z = dot(jnp.concatenate(lhs, axis=0), z_main[...])
            x = dot(a_edge[...], jnp.concatenate(rhs, axis=1))
            for i, field, ny, slot in planes(p):
                put(
                    i,
                    z[16 * slot : 16 * slot + 16]
                    + x[:, 128 * slot : 128 * slot + 128]
                    + eo[16 * p : 16 * p + 16, 128 * slot : 128 * slot + 128],
                )

        for p in range(9):
            one(p)

    for p in range(9):
        e, m = pq[p], mid(pq, p)
        k = pack_kappa(kappa, p) * (dt / second_part)
        el[16 * p : 16 * p + 16, :] = across(k * m, mid(pvq, 1) * m)
    eo[...] = dot(el[...], z_pack[...])
    for p in range(9):
        e, m = pq[p], mid(pq, p)
        k = pack_kappa(kappa, p) * (dt / second_part)
        x = dot(a_edge[...], down_rows(k * e, pvq[0] * e))
        new = m + x + eo[16 * p : 16 * p + 16, 512:640]
        ps1[p, 0:8, :] = new[0:8]
        ps1[p, 24:32, :] = new[8:16]
    ng = jnp.concatenate([zeros, packs[10, 0:4, :], packs[10, 60:64, :], zeros], axis=0)
    src = pack_sources(lambda k: mid(pq, k), ng, dt)
    for k in range(7):
        ps1[k, 0:8, :] += src[k][0:8]
        ps1[k, 24:32, :] += src[k][8:16]

    def put_one(i, rate):
        new = mid(q, i) + rate
        s1[i, 0:8, :] = new[0:8]
        s1[i, 24:32, :] = new[8:16]

    stage(q, vq, dt, put_one)
    for ny in range(2):
        near, far = above[39 + ny], below[39 + ny]
        nucl = jnp.concatenate([near[0:4], fields[40 + ny, 0:4, :], fields[40 + ny, 60:64, :], far[0:4]], axis=0)
        grow = jnp.concatenate([near[4:8], fields[42 + ny, 0:4, :], fields[42 + ny, 60:64, :], far[4:8]], axis=0)
        src = sources(lambda k: mid(q, 2 * k + ny), nucl, grow, dt)
        for k in range(7):
            s1[2 * k + ny, 0:8, :] += src[k][0:8]
            s1[2 * k + ny, 24:32, :] += src[k][8:16]

    scale = 0.5 * dt
    for p in range(9):
        m = mid(ps1, p)
        k = pack_kappa(kappa, p) * (scale / second_part)
        el[16 * p : 16 * p + 16, :] = across(k * m, (0.5 * pvq[1, 8:24, :]) * m)
    eo[:, 0:512] = dot(el[...], z_pack[:, 0:512])

    def put_two(i, rate):
        own = jnp.concatenate([fields[i, 0:8, :], fields[i, 56:64, :]], axis=0)
        done[i] = 0.5 * (own + mid(s1, i)) + rate

    stage(s1, v1, scale, put_two)
    for ny in range(2):
        nucl = jnp.concatenate([fields[40 + ny, 0:8, :], fields[40 + ny, 56:64, :]], axis=0)
        grow = jnp.concatenate([fields[42 + ny, 0:8, :], fields[42 + ny, 56:64, :]], axis=0)
        src = sources(lambda k: mid(s1, 2 * k + ny), nucl, grow, scale)
        for k in range(7):
            done[2 * k + ny] += src[k]
    last = [
        pltpu.make_async_copy(
            done.at[pl.ds(at, size), pl.ds(8 * side, 8)],
            out.at[pl.ds(0, size), pl.ds(56 * side, 8)],
            sems.at[2 + 2 * n + side],
        )
        for n, (out, at, size) in enumerate(outs)
        for side in range(2)
    ]
    for copy in last:
        copy.start()
    for copy in copies + last:
        copy.wait()


def call(kernel, outs, cost, mib=24, **kw):
    return pl.pallas_call(
        kernel,
        out_shape=[jax.ShapeDtypeStruct(o, F32) for o in outs],
        cost_estimate=pl.CostEstimate(flops=cost, bytes_accessed=cost // 4, transcendentals=0),
        compiler_params=pltpu.CompilerParams(vmem_limit_bytes=mib * 2**20),
        **kw,
    )


def send(value, axis, by):
    peers = lax.axis_size(axis)
    return lax.ppermute(value, axis, [(i, (i + by) % peers) for i in range(peers)])


def body(moments, scalars, velocity, diffusivity, nucleation, growth):
    vmem = pl.BlockSpec(memory_space=pltpu.VMEM)
    smem = pl.BlockSpec(memory_space=pltpu.SMEM)
    hbm = pl.BlockSpec(memory_space=pltpu.HBM)
    tiles = lambda *lead: pltpu.VMEM(lead + (128,), F32)
    flat = [x.reshape(-1, 64, 128) for x in (moments, scalars, velocity, nucleation, growth)]
    a_rows, a_edge, z_main, z_pack = (jnp.asarray(m) for m in matrices())

    zl, zr = call(
        pack_z,
        [(3, 64, 128), (3, 64, 128)],
        10**6,
        56,
        in_specs=[hbm] * 5,
        out_specs=[vmem] * 2,
        scratch_shapes=[tiles(44, 64), pltpu.SemaphoreType.DMA((10,))],
    )(*flat)
    from_right = send(zl, "gz", -1)
    from_left = send(zr, "gz", 1)
    fields, own, up, down = call(
        prepare, [(44, 64, 128), (11, 64, 128), (43, 8, 128), (43, 8, 128)], 10**6
    )(*flat)
    up, down = call(
        corners,
        [(43, 8, 128), (43, 8, 128)],
        10**6,
        in_specs=[vmem] * 2 + [pl.BlockSpec(memory_space=pl.ANY)] * 2,
        out_specs=[pl.BlockSpec(memory_space=pl.ANY)] * 2,
        input_output_aliases={2: 0, 3: 1},
        scratch_shapes=[tiles(2, 2, 8), pltpu.SemaphoreType.DMA((2,))],
    )(from_left, from_right, up, down)
    above = send(up, "gx", 1)
    below = send(down, "gx", -1)
    packs, q1, pq1, half = call(
        interior,
        [(11, 64, 128), (36, 64, 128), (9, 64, 128), (36, 64, 128)],
        10**8,
        in_specs=[smem] + [vmem] * 7,
        scratch_shapes=[
            tiles(2, 64), tiles(2, 64), tiles(64), tiles(64), pltpu.VMEM((576, 512), BF16), pltpu.VMEM((576, 640), F32),
        ],
    )(diffusivity, fields, own, from_left, from_right, a_rows, z_main, z_pack)
    out_mom, out_sca = call(
        edges,
        [(12, 64, 128), (24, 64, 128)],
        10**8,
        in_specs=[smem] + [vmem] * 10,
        out_specs=[hbm] * 2,
        scratch_shapes=[
            tiles(36, 32), tiles(36, 32), tiles(4, 32), tiles(4, 32), tiles(10, 32), tiles(9, 32), tiles(2, 32),
            pltpu.VMEM((144, 512), BF16), pltpu.VMEM((144, 640), F32), tiles(36, 16), pltpu.SemaphoreType.DMA((6,)),
        ],
    )(diffusivity, fields, packs, q1, pq1, half, above, below, a_edge, z_main, z_pack)
    return out_mom.reshape(moments.shape), out_sca.reshape(scalars.shape)


def solution(mesh):
    return jax.shard_map(
        body,
        mesh=mesh,
        in_specs=(
            P(None, None, "gx", "gz"),
            P(None, None, "gx", "gz"),
            P(None, None, "gx", "gz"),
            P(),
            P(None, "gx", "gz"),
            P(None, "gx", "gz"),
        ),
        out_specs=(P(None, None, "gx", "gz"), P(None, None, "gx", "gz")),
        check_vma=False,
    )
```

```python
import numpy as np

import jax
import jax.numpy as jnp
from jax import lax
from jax.experimental import pallas as pl
from jax.experimental.pallas import tpu as pltpu
from jax.sharding import PartitionSpec as P

first_whole, first_part = (672.0, -168.0, 32.0, -3.0), 840.0
second_whole, second_part = (8064.0, -1008.0, 128.0, -9.0), 5040.0
centre_x, centre_z = -28672.0, -28.0
time_step = 0.25

F32, BF16 = jnp.float32, jnp.bfloat16


def band(targets, sources, centre):
    gap = np.asarray(sources)[None, :] - np.asarray(targets)[:, None]
    second = np.where(gap == 0, centre, 0.0)
    first = np.zeros(gap.shape)
    for m in range(1, 5):
        second = second + second_whole[m - 1] * (abs(gap) == m)
        first = first - first_whole[m - 1] * ((gap == m) * 1.0 - (gap == -m))
    return second, first


def matrices():
    both = lambda pair, axis: np.concatenate([pair[0], pair[0], pair[1], pair[1]], axis=axis).astype(BF16)
    rows, cols = np.arange(64), np.arange(128)
    a_rows = both(band(rows, rows, centre_x), 1)
    place, away = np.arange(32), 1000
    part = np.concatenate([place[:16], away + place[16:]])
    a_edge = both(band(np.concatenate([part[4:12], part[20:28]]), part, centre_x), 1)
    z_main = both(tuple(m.T for m in band(cols, cols, centre_z)), 0)
    slot_col = np.concatenate([np.arange(-8, 8), np.arange(120, 136)])
    beyond = (slot_col < 0) | (slot_col >= 128)
    to_planes = []
    for matrix in band(cols, slot_col, 0.0):
        wide = np.zeros((128, 512))
        for s in range(4):
            wide[32 * s : 32 * s + 32, 128 * s : 128 * s + 128] = (matrix * beyond[None, :]).T
        to_planes.append(wide)
    lane = np.arange(128)
    in_slot = [m.T * (lane[:, None] // 16 == lane[None, :] // 16) for m in band(lane, lane, centre_z)]
    z_pack = both(tuple(np.concatenate([w, o], axis=1) for w, o in zip(to_planes, in_slot)), 0)
    return a_rows, a_edge, z_main, z_pack


def lanes(shape=(8, 128)):
    return lax.broadcasted_iota(jnp.int32, shape, len(shape) - 1)


def roll(x, by):
    by = by % 128
    return x if by == 0 else pltpu.roll(x, by, 1)


def split(x):
    high = x.astype(BF16)
    return high, (x - high.astype(F32)).astype(BF16)


def dot(a, b):
    return jnp.dot(a, b, preferred_element_type=F32)


def plane_of(p, s):
    c, ny = s // 2, s % 2
    return 2 * (p + 9 * c) + ny if p < 9 else 4 * p + s


def odd_of(axis):
    return lax.axis_index(axis) % 2


def z_messages(fields, r, t):
    pair, odd = lanes() // 16, (lanes() // 8) % 2 == 1
    tile = [None, None]
    for j in range(4 if t < 2 else 3):
        for s in range(4):
            c = 2 * s + j // 2
            one = roll(fields[plane_of(4 * t + j, s), r : r + 8, :], 16 * c + 8)
            half = tile[j % 2]
            tile[j % 2] = one if half is None else jnp.where(pair == c, one, half)
    return jnp.where(odd, tile[1], roll(tile[0], -8)), jnp.where(odd, roll(tile[1], 8), tile[0])


def pack_z(mom, sca, vel, nuc, gro, far, near, fields, sems):
    parts = [
        [(mom, 0, 0, 8), (sca, 6, 18, 8)],
        [(mom, 8, 8, 4), (sca, 0, 12, 4), (sca, 14, 26, 8)],
        [(sca, 4, 16, 2), (sca, 22, 34, 2), (vel, 0, 36, 4), (nuc, 0, 40, 2), (gro, 0, 42, 2)],
    ]
    copies, n = [], 0
    for part in parts:
        copies.append([])
        for src, at, to, size in part:
            copies[-1].append(
                pltpu.make_async_copy(src.at[pl.ds(at, size)], fields.at[pl.ds(to, size)], sems.at[n])
            )
            copies[-1][-1].start()
            n += 1
    right = odd_of("gz") == 0
    for t in range(3):
        for copy in copies[t]:
            copy.wait()
        for r in range(0, 64, 8):
            zl, zr = z_messages(fields, r, t)
            far[t, r : r + 8, :] = jnp.where(right, zl, zr)
            near[t, r : r + 8, :] = jnp.where(right, zr, zl)


def x_messages(fields, z_near, first, second, near):
    near[...] = z_near[...]
    odd = odd_of("gx") == 1
    for k, msg in enumerate((first, second)):
        low = odd if k == 0 else jnp.logical_not(odd)
        at = pl.ds(pl.multiple_of(jnp.where(low, 0, 56), 8), 8)
        for i in range(38):
            msg[i] = fields[i, at, :]
        for n, i in enumerate((38, 39, 40, 42, 41, 43)):
            tile = fields[i, at, :]
            tile = jnp.where(low, tile[0:4], tile[4:8])
            msg[38 + n // 2, 4 * (n % 2) : 4 * (n % 2) + 4, :] = tile


def own_packs(fields, own):
    sub = lanes() // 8
    for p in range(11):
        for r in range(0, 64, 8):
            e = jnp.zeros((8, 128), F32)
            for s in range(4):
                tile = fields[plane_of(p, s), r : r + 8, :]
                e = jnp.where(sub == 4 * s + 1, roll(tile, 32 * s + 8), e)
                e = jnp.where(sub == 4 * s + 2, roll(tile, 32 * s + 24), e)
            own[p, r : r + 8, :] = e


def corners(near, far, part, first, second):
    del part
    right = odd_of("gz") == 0
    odd = odd_of("gx") == 1
    inner = lanes((4, 128)) % 8 < 4
    first[1, 4:8, :] = second[1, 4:8, :] = jnp.zeros((4, 128), F32)
    for t in range(3):
        at = slice(4 * (t % 2), 4 * (t % 2) + 4)
        part = []
        for rows in (slice(0, 4), slice(60, 64)):
            from_near, from_far = near[t, rows, :], far[t, rows, :]
            from_left = jnp.where(right, from_far, from_near)
            part.append(jnp.where(inner, jnp.where(right, from_near, from_far), from_left))
        first[t // 2, at, :] = jnp.where(odd, part[0], part[1])
        second[t // 2, at, :] = jnp.where(odd, part[1], part[0])


def fill_packs(own, near, far, packs):
    sub = (lanes((64, 128)) // 8) % 4
    right = odd_of("gz") == 0
    for t in range(3):
        from_left = jnp.where(right, far[t], near[t])
        from_right = jnp.where(right, near[t], far[t])
        for j in range(4 if t < 2 else 3):
            p = 4 * t + j
            e = jnp.where(sub == 0, roll(from_left, -8 * j), own[p])
            packs[p] = jnp.where(sub == 3, roll(from_right, 24 - 8 * j), e)


def sources(get, nucl, grow, scale):
    y = get(6)
    birth = nucl * y * y
    moms = [get(k) for k in range(6)]
    half = (0.5 * scale) * birth
    sink = (0.3 * scale) * moms[0]
    out = []
    for k in range(6):
        s = half - sink * moms[k]
        if k:
            s = s + ((scale * k / 3.0) * grow) * moms[k - 1]
        out.append(s)
    return out + [(-0.2 * scale) * birth]


def pack_sources(get, ng, scale):
    low = lanes(ng.shape) < 64
    nucl = jnp.where(low, ng, 0.0)
    grow = jnp.where(low, roll(ng, 64), 0.0)
    y = get(6)
    birth = nucl * y * y
    moms = [get(k) for k in range(6)]
    half = (0.5 * scale) * birth
    sink = jnp.where(low, (0.3 * scale) * moms[0], 0.0)
    out = []
    for k in range(6):
        s = half - sink * moms[k]
        if k:
            s = s + ((scale * k / 3.0) * grow) * moms[k - 1]
        out.append(s)
    return out + [(-0.2 * scale) * birth]


def pack_velocity(tile):
    low = lanes(tile.shape) < 64
    other = roll(tile, 64)
    return jnp.where(low, tile, other), jnp.where(low, other, tile)


def pack_kappa(kappa, p):
    return jnp.where(lanes((1, 128)) < 64, kappa[p], kappa[p + 9])


def planes(p):
    for slot in range(4):
        field, ny = p + 9 * (slot // 2), slot % 2
        yield 2 * field + ny, field, ny, slot


def across(kq, g):
    return jnp.concatenate([*split(kq), *split(g)], axis=1)


def down_rows(kq, f):
    return jnp.concatenate([*split(kq), *split(f)], axis=0)


GROUP = 3


def groups(fn):
    def step(i, _):
        for k in range(GROUP):
            fn(i * GROUP + k)
        return _

    lax.fori_loop(0, 9 // GROUP, step, 0)


def plane_velocities(fields, us, ws, scale):
    for ny in range(2):
        us[ny] = fields[36 + ny] * (scale / first_part)
        ws[ny] = fields[38 + ny] * (scale / first_part)


def first_stage(kappa, fields, a_rows, z_main, part, own, us, ws):
    dt = time_step
    own_packs(fields, own)
    plane_velocities(fields, us, ws, dt)

    def one(p):
        lhs, rhs = [], []
        for i, field, ny, slot in planes(p):
            v = fields[i]
            kq = (kappa[field] * (dt / second_part)) * v
            lhs.append(across(kq, ws[ny] * v))
            rhs.append(down_rows(kq, us[ny] * v))
        z = dot(jnp.concatenate(lhs, axis=0), z_main[...])
        x = [dot(a_rows[...], jnp.concatenate(rhs[c : c + 2], axis=1)) for c in (0, 2)]
        for i, field, ny, slot in planes(p):
            part[i] = fields[i] + z[64 * slot : 64 * slot + 64] + x[slot // 2][:, 128 * ny : 128 * ny + 128]

    groups(one)
    for ny in range(2):
        src = sources(lambda k: fields[2 * k + ny], fields[40 + ny], fields[42 + ny], dt)
        for k in range(7):
            part[2 * k + ny] += src[k]


def interior(
    kappa, fields, part, own, near, far, a_rows, z_main, z_pack, packs, q1, pq1, half,
    us, ws, pus, pws, el, eo,
):
    fill_packs(own, near, far, packs)
    dt, scale = time_step, 0.5 * time_step
    pu, pw = pack_velocity(packs[9])
    pus[...] = pu * (dt / first_part)
    pws[...] = pw * (dt / first_part)
    for p in range(9):
        e = packs[p]
        kq = (pack_kappa(kappa, p) * (dt / second_part)) * e
        el[64 * p : 64 * p + 64, :] = across(kq, pws[...] * e)
    eo[...] = dot(el[...], z_pack[...])
    for p in range(9):
        e = packs[p]
        kq = (pack_kappa(kappa, p) * (dt / second_part)) * e
        x = dot(a_rows[...], down_rows(kq, pus[...] * e))
        pq1[p] = e + x + eo[64 * p : 64 * p + 64, 512:640]
    src = pack_sources(lambda k: packs[k], packs[10], dt)
    for k in range(7):
        pq1[k] += src[k]
    for p in range(9):
        for i, field, ny, slot in planes(p):
            q1[i] = part[i] + eo[64 * p : 64 * p + 64, 128 * slot : 128 * slot + 128]

    plane_velocities(fields, us, ws, scale)
    for p in range(9):
        e = pq1[p, 8:56, :]
        kq = (pack_kappa(kappa, p) * (scale / second_part)) * e
        el[48 * p : 48 * p + 48, :] = across(kq, (0.5 * pws[8:56, :]) * e)
    eo[0:432, 0:512] = dot(el[0:432, :], z_pack[:, 0:512])

    def two(p):
        lhs, rhs = [], []
        for i, field, ny, slot in planes(p):
            v = q1[i]
            kq = (kappa[field] * (scale / second_part)) * v
            mid = v[8:56]
            lhs.append(across(kq[8:56], ws[ny, 8:56, :] * mid))
            rhs.append(down_rows(kq, us[ny] * v))
        z = dot(jnp.concatenate(lhs, axis=0), z_main[...])
        x = [dot(a_rows[8:56, :], jnp.concatenate(rhs[c : c + 2], axis=1)) for c in (0, 2)]
        for i, field, ny, slot in planes(p):
            half[i, 8:56, :] = (
                0.5 * (fields[i, 8:56, :] + q1[i, 8:56, :])
                + z[48 * slot : 48 * slot + 48]
                + x[slot // 2][:, 128 * ny : 128 * ny + 128]
                + eo[pl.ds(48 * p, 48), 128 * slot : 128 * slot + 128]
            )

    groups(two)
    for ny in range(2):
        src = sources(
            lambda k: q1[2 * k + ny, 8:56, :], fields[40 + ny, 8:56, :], fields[42 + ny, 8:56, :], scale
        )
        for k in range(7):
            half[2 * k + ny, 8:56, :] += src[k]


def edges(
    kappa, fields, packs, q1, pq1, half, first, second, first_corner, second_corner, a_edge, z_main, z_pack, out_mom, out_sca,
    q, s1, vq, v1, pq, ps1, pvq, el, eo, done, sems,
):
    outs = [(out_mom, 0, 12), (out_sca, 12, 24)]
    copies = [
        pltpu.make_async_copy(
            half.at[pl.ds(at, size), pl.ds(8, 48)], out.at[pl.ds(0, size), pl.ds(8, 48)], sems.at[n]
        )
        for n, (out, at, size) in enumerate(outs)
    ]
    for copy in copies:
        copy.start()
    dt = time_step
    top, low = slice(4, 12), slice(20, 28)
    mid = lambda ref, *at: jnp.concatenate([ref[*at, top, :], ref[*at, low, :]], axis=0)

    odd = odd_of("gx") == 1
    above = lambda i, at=slice(0, 8): jnp.where(odd, first[i, at, :], second[i, at, :])
    below = lambda i, at=slice(0, 8): jnp.where(odd, second[i, at, :], first[i, at, :])
    for i in range(36):
        q[i, 0:8, :] = above(i)
        q[i, 8:16, :] = fields[i, 0:8, :]
        q[i, 16:24, :] = fields[i, 56:64, :]
        q[i, 24:32, :] = below(i)
        s1[i, 8:16, :] = q1[i, 4:12, :]
        s1[i, 16:24, :] = q1[i, 52:60, :]
    one, two = dt / first_part, 0.5 * dt / first_part
    for i in range(4):
        k = 36 + i
        if i < 2:
            vq[i, 0:8, :] = above(k) * one
            vq[i, 24:32, :] = below(k) * one
        else:
            at = slice(4 * (i % 2), 4 * (i % 2) + 4)
            vq[i, 0:4, :] = vq[i, 28:32, :] = jnp.zeros((4, 128), F32)
            vq[i, 4:8, :] = above(38, at) * one
            vq[i, 24:28, :] = below(38, at) * one
        vq[i, 8:16, :] = fields[k, 0:8, :] * one
        vq[i, 16:24, :] = fields[k, 56:64, :] * one
        v1[i, 0:4, :] = vq[i, 4:8, :] * 0.5
        v1[i, 4:16, :] = fields[k, 0:12, :] * two
        v1[i, 16:28, :] = fields[k, 52:64, :] * two
        v1[i, 28:32, :] = vq[i, 24:28, :] * 0.5
    zeros = jnp.zeros((4, 128), F32)
    lane = lanes() % 32
    is_left, is_right = (lane >= 4) & (lane < 8), (lane >= 24) & (lane < 28)
    for p in range(10):
        t, j = p // 4, p % 4
        at = slice(4 * (t % 2), 4 * (t % 2) + 4)
        one_c, two_c = first_corner[t // 2, at, :], second_corner[t // 2, at, :]
        corner = jnp.concatenate([jnp.where(odd, one_c, two_c), jnp.where(odd, two_c, one_c)], axis=0)
        corner = jnp.where(
            is_left, roll(corner, -8 * j), jnp.where(is_right, roll(corner, 24 - 8 * j), 0.0)
        )
        pq[p, 0:4, :] = zeros
        pq[p, 4:8, :] = corner[0:4]
        pq[p, 8:16, :] = packs[p, 0:8, :]
        pq[p, 16:24, :] = packs[p, 56:64, :]
        pq[p, 24:28, :] = corner[4:8]
        pq[p, 28:32, :] = zeros
    for p in range(9):
        ps1[p, 8:16, :] = pq1[p, 4:12, :]
        ps1[p, 16:24, :] = pq1[p, 52:60, :]
    pu, pw = pack_velocity(pq[9])
    pvq[0], pvq[1] = pu * one, pw * one

    def stage(src, vel, scale, put):
        def one(p):
            lhs, rhs = [], []
            for i, field, ny, slot in planes(p):
                k = kappa[field] * (scale / second_part)
                v, m = src[i], mid(src, i)
                lhs.append(across(k * m, mid(vel, 2 + ny) * m))
                rhs.append(down_rows(k * v, vel[ny] * v))
            z = dot(jnp.concatenate(lhs, axis=0), z_main[...])
            x = dot(a_edge[...], jnp.concatenate(rhs, axis=1))
            for i, field, ny, slot in planes(p):
                put(
                    i,
                    z[16 * slot : 16 * slot + 16]
                    + x[:, 128 * slot : 128 * slot + 128]
                    + eo[16 * p : 16 * p + 16, 128 * slot : 128 * slot + 128],
                )

        for p in range(9):
            one(p)

    for p in range(9):
        e, m = pq[p], mid(pq, p)
        k = pack_kappa(kappa, p) * (dt / second_part)
        el[16 * p : 16 * p + 16, :] = across(k * m, mid(pvq, 1) * m)
    eo[...] = dot(el[...], z_pack[...])
    for p in range(9):
        e, m = pq[p], mid(pq, p)
        k = pack_kappa(kappa, p) * (dt / second_part)
        x = dot(a_edge[...], down_rows(k * e, pvq[0] * e))
        new = m + x + eo[16 * p : 16 * p + 16, 512:640]
        ps1[p, 0:8, :] = new[0:8]
        ps1[p, 24:32, :] = new[8:16]
    ng = jnp.concatenate([zeros, packs[10, 0:4, :], packs[10, 60:64, :], zeros], axis=0)
    src = pack_sources(lambda k: mid(pq, k), ng, dt)
    for k in range(7):
        ps1[k, 0:8, :] += src[k][0:8]
        ps1[k, 24:32, :] += src[k][8:16]

    def put_one(i, rate):
        new = mid(q, i) + rate
        s1[i, 0:8, :] = new[0:8]
        s1[i, 24:32, :] = new[8:16]

    stage(q, vq, dt, put_one)
    for ny in range(2):
        near, far = above(39 + ny), below(39 + ny)
        nucl = jnp.concatenate([near[0:4], fields[40 + ny, 0:4, :], fields[40 + ny, 60:64, :], far[0:4]], axis=0)
        grow = jnp.concatenate([near[4:8], fields[42 + ny, 0:4, :], fields[42 + ny, 60:64, :], far[4:8]], axis=0)
        src = sources(lambda k: mid(q, 2 * k + ny), nucl, grow, dt)
        for k in range(7):
            s1[2 * k + ny, 0:8, :] += src[k][0:8]
            s1[2 * k + ny, 24:32, :] += src[k][8:16]

    scale = 0.5 * dt
    for p in range(9):
        m = mid(ps1, p)
        k = pack_kappa(kappa, p) * (scale / second_part)
        el[16 * p : 16 * p + 16, :] = across(k * m, (0.5 * pvq[1, 8:24, :]) * m)
    eo[:, 0:512] = dot(el[...], z_pack[:, 0:512])

    def put_two(i, rate):
        own = jnp.concatenate([fields[i, 0:8, :], fields[i, 56:64, :]], axis=0)
        done[i] = 0.5 * (own + mid(s1, i)) + rate

    stage(s1, v1, scale, put_two)
    for ny in range(2):
        nucl = jnp.concatenate([fields[40 + ny, 0:8, :], fields[40 + ny, 56:64, :]], axis=0)
        grow = jnp.concatenate([fields[42 + ny, 0:8, :], fields[42 + ny, 56:64, :]], axis=0)
        src = sources(lambda k: mid(s1, 2 * k + ny), nucl, grow, scale)
        for k in range(7):
            done[2 * k + ny] += src[k]
    last = [
        pltpu.make_async_copy(
            done.at[pl.ds(at, size), pl.ds(8 * side, 8)],
            out.at[pl.ds(0, size), pl.ds(56 * side, 8)],
            sems.at[2 + 2 * n + side],
        )
        for n, (out, at, size) in enumerate(outs)
        for side in range(2)
    ]
    for copy in last:
        copy.start()
    for copy in copies + last:
        copy.wait()


def call(kernel, outs, cost, mib=24, **kw):
    return pl.pallas_call(
        kernel,
        out_shape=[jax.ShapeDtypeStruct(o, F32) for o in outs],
        cost_estimate=pl.CostEstimate(flops=cost, bytes_accessed=cost // 4, transcendentals=0),
        compiler_params=pltpu.CompilerParams(vmem_limit_bytes=mib * 2**20),
        **kw,
    )


def swap(value, axis, far):
    peers = lax.axis_size(axis)
    other = lambda i: (((i + far) ^ 1) - far) % peers
    return lax.ppermute(value, axis, [(i, other(i)) for i in range(peers)])


def body(moments, scalars, velocity, diffusivity, nucleation, growth):
    vmem = pl.BlockSpec(memory_space=pltpu.VMEM)
    smem = pl.BlockSpec(memory_space=pltpu.SMEM)
    hbm = pl.BlockSpec(memory_space=pltpu.HBM)
    tiles = lambda *lead: pltpu.VMEM(lead + (128,), F32)
    flat = [
        pltpu.with_memory_space_constraint(x.reshape(-1, 64, 128), pltpu.HBM)
        for x in (moments, scalars, velocity, nucleation, growth)
    ]
    a_rows, a_edge, z_main, z_pack = (jnp.asarray(m) for m in matrices())

    z_far, z_near, fields = call(
        pack_z,
        [(3, 64, 128), (3, 64, 128), (44, 64, 128)],
        10**6,
        in_specs=[hbm] * 5,
        out_specs=[vmem] * 3,
        scratch_shapes=[pltpu.SemaphoreType.DMA((10,))],
    )(*flat)
    far = swap(z_far, "gz", 1)
    x_first, x_second, z_near = call(x_messages, [(41, 8, 128), (41, 8, 128), (3, 64, 128)], 10**5)(fields, z_near)
    near = swap(z_near, "gz", 0)
    part, own = call(
        first_stage,
        [(36, 64, 128), (11, 64, 128)],
        10**7,
        in_specs=[smem] + [vmem] * 3,
        scratch_shapes=[tiles(2, 64), tiles(2, 64)],
    )(diffusivity, fields, a_rows, z_main)
    second = swap(x_second, "gx", 1)
    first = swap(x_first, "gx", 0)
    c_first, c_second = call(corners, [(2, 8, 128)] * 2, 10**6)(near, far, part)
    second_corner = swap(c_second, "gx", 1)
    first_corner = swap(c_first, "gx", 0)
    packs, q1, pq1, half = call(
        interior,
        [(11, 64, 128), (36, 64, 128), (9, 64, 128), (36, 64, 128)],
        10 * 10**8,
        in_specs=[smem] + [vmem] * 8,
        scratch_shapes=[
            tiles(2, 64), tiles(2, 64), tiles(64), tiles(64), pltpu.VMEM((576, 512), BF16), pltpu.VMEM((576, 640), F32),
        ],
    )(diffusivity, fields, part, own, near, far, a_rows, z_main, z_pack)
    out_mom, out_sca = call(
        edges,
        [(12, 64, 128), (24, 64, 128)],
        10**8,
        in_specs=[smem] + [vmem] * 12,
        out_specs=[hbm] * 2,
        scratch_shapes=[
            tiles(36, 32), tiles(36, 32), tiles(4, 32), tiles(4, 32), tiles(10, 32), tiles(9, 32), tiles(2, 32),
            pltpu.VMEM((144, 512), BF16), pltpu.VMEM((144, 640), F32), tiles(36, 16), pltpu.SemaphoreType.DMA((6,)),
        ],
    )(
            diffusivity, fields, packs, q1, pq1, half, first, second, first_corner, second_corner, a_edge, z_main, z_pack
        )
    return out_mom.reshape(moments.shape), out_sca.reshape(scalars.shape)


def solution(mesh):
    return jax.shard_map(
        body,
        mesh=mesh,
        in_specs=(
            P(None, None, "gx", "gz"),
            P(None, None, "gx", "gz"),
            P(None, None, "gx", "gz"),
            P(),
            P(None, "gx", "gz"),
            P(None, "gx", "gz"),
        ),
        out_specs=(P(None, None, "gx", "gz"), P(None, None, "gx", "gz")),
        check_vma=False,
    )
```

```python
import numpy as np

import jax
import jax.numpy as jnp
from jax import lax
from jax.experimental import pallas as pl
from jax.experimental.pallas import tpu as pltpu
from jax.sharding import PartitionSpec as P

first_whole, first_part = (672.0, -168.0, 32.0, -3.0), 840.0
second_whole, second_part = (8064.0, -1008.0, 128.0, -9.0), 5040.0
centre_x, centre_z = -28672.0, -28.0
time_step = 0.25

F32, BF16 = jnp.float32, jnp.bfloat16


def band(targets, sources, centre):
    gap = np.asarray(sources)[None, :] - np.asarray(targets)[:, None]
    second = np.where(gap == 0, centre, 0.0)
    first = np.zeros(gap.shape)
    for m in range(1, 5):
        second = second + second_whole[m - 1] * (abs(gap) == m)
        first = first - first_whole[m - 1] * ((gap == m) * 1.0 - (gap == -m))
    return second, first


rows_h = [64, 65, 66, 67, -4, -3, -2, -1]
rows_o = [-8, -7, -6, -5, 68, 69, 70, 71]
rows_a = [0, 1, 2, 3, 60, 61, 62, 63]
rows_b = [56, 57, 58, 59, 4, 5, 6, 7]
rows_c = [8, 9, 10, 11, 52, 53, 54, 55]


def matrices():
    both = lambda pair, axis: np.concatenate([pair[0], pair[0], pair[1], pair[1]], axis=axis)
    rows, cols = np.arange(64), np.arange(128)
    a_rows = both(band(rows, rows, centre_x), 1)
    far = band(rows_h + rows_a, rows_h + rows_o, centre_x)
    own = [m * (np.arange(16) < 8)[:, None] for m in band(rows_h + rows_a, rows_a, centre_x)]
    a_one = np.concatenate([both(far, 1), own[0], own[1], own[0], own[1]], axis=1)
    a_two = np.concatenate(
        [both(band(rows_a + rows_b, src, centre_x), 1) for src in (rows_a + rows_b, rows_h + rows_c)], axis=1
    )
    corner = [np.concatenate([m, 0 * m]) for m in band(rows_a, rows_h, centre_x)]
    a_corner = np.concatenate(corner + corner, axis=1)
    z_main = both([m.T for m in band(cols, cols, centre_z)], 0)
    blocks = lambda pair: both([np.kron(np.eye(16), m.T) for m in pair], 0)
    outer = [128, 129, 130, 131, -4, -3, -2, -1]
    z_outer = np.concatenate(
        [blocks(band(outer, np.arange(at, at + 8), centre_z)) for at in (-8, 0, 128, 120)]
    )
    z_inner = blocks(band([124, 125, 126, 127, 0, 1, 2, 3], outer, centre_z))
    return [m.astype(BF16) for m in (a_rows, a_one, a_two, a_corner, z_main, z_outer, z_inner)]


def lanes(shape=(8, 128)):
    return lax.broadcasted_iota(jnp.int32, shape, len(shape) - 1)


def roll(x, by):
    by = by % 128
    return x if by == 0 else pltpu.roll(x, by, 1)


def split(x):
    high = x.astype(BF16)
    return high, (x - high.astype(F32)).astype(BF16)


def dot(a, b):
    return jnp.dot(a, b, preferred_element_type=F32)


def plane_of(p, s):
    c, ny = s // 2, s % 2
    return 2 * (p + 9 * c) + ny if p < 9 else 4 * p + s


def odd_of(axis):
    return lax.axis_index(axis) % 2


def z_messages(fields, r, t):
    pair, odd = lanes() // 16, (lanes() // 8) % 2 == 1
    tile = [None, None]
    for j in range(4 if t < 2 else 3):
        for s in range(4):
            c = 2 * s + j // 2
            one = roll(fields[plane_of(4 * t + j, s), r : r + 8, :], 16 * c + 8)
            half = tile[j % 2]
            tile[j % 2] = one if half is None else jnp.where(pair == c, one, half)
    return jnp.where(odd, tile[1], roll(tile[0], -8)), jnp.where(odd, roll(tile[1], 8), tile[0])


def pack_z(mom, sca, vel, nuc, gro, far, near, fields, sems):
    parts = [
        [(mom, 0, 0, 8), (sca, 6, 18, 8)],
        [(mom, 8, 8, 4), (sca, 0, 12, 4), (sca, 14, 26, 8)],
        [(sca, 4, 16, 2), (sca, 22, 34, 2), (vel, 0, 36, 4), (nuc, 0, 40, 2), (gro, 0, 42, 2)],
    ]
    copies, n = [], 0
    for part in parts:
        copies.append([])
        for src, at, to, size in part:
            copies[-1].append(
                pltpu.make_async_copy(src.at[pl.ds(at, size)], fields.at[pl.ds(to, size)], sems.at[n])
            )
            copies[-1][-1].start()
            n += 1
    right = odd_of("gz") == 0
    for t in range(3):
        for copy in copies[t]:
            copy.wait()
        for r in range(0, 64, 8):
            zl, zr = z_messages(fields, r, t)
            far[t, r : r + 8, :] = jnp.where(right, zl, zr)
            near[t, r : r + 8, :] = jnp.where(right, zr, zl)


def halves(first):
    return (lax.broadcasted_iota(jnp.int32, (8, 128), 0) + 4 * first) % 8 >= 4


def x_messages(fields, z_near, first, second, near):
    near[...] = z_near[...]
    odd = odd_of("gx") == 1
    for k, msg in enumerate((first, second)):
        low = odd if k == 0 else jnp.logical_not(odd)
        at = pl.ds(pl.multiple_of(jnp.where(low, 0, 56), 8), 8)
        for i in range(38):
            msg[i] = fields[i, at, :]
        keep = halves(low.astype(jnp.int32))
        for n, (i, j) in enumerate(((38, 39), (40, 42), (41, 43))):
            msg[38 + n] = jnp.where(keep, fields[i, at, :], pltpu.roll(fields[j, at, :], 4, 0))


def outer_tile(from_left, from_right):
    return jnp.where(lanes(from_left.shape) % 8 >= 4, from_left, from_right)


def sides(near, far):
    right = odd_of("gz") == 0
    return jnp.where(right, far, near), jnp.where(right, near, far)


def corners(near, far, part, first, second):
    del part
    odd = odd_of("gx") == 1
    for k, msg in enumerate((first, second)):
        low = odd if k == 0 else jnp.logical_not(odd)
        at = pl.ds(pl.multiple_of(jnp.where(low, 0, 56), 8), 8)
        keep = halves(low.astype(jnp.int32))
        tile = [outer_tile(*sides(near[t, at, :], far[t, at, :])) for t in range(3)]
        msg[0] = jnp.where(keep, tile[0], pltpu.roll(tile[1], 4, 0))
        msg[1] = jnp.where(keep, tile[2], 0.0)


def spread(tile, j):
    x = jnp.where((lanes(tile.shape) // 8) % 4 == j, tile, 0.0)
    x = x + roll(x, -8 if j % 2 else 8)
    return x + roll(x, -16 if j >= 2 else 16)


def block_velocity(tile):
    x = spread(tile, 1)
    low, other = lanes(tile.shape) < 64, roll(x, 64)
    return jnp.where(low, x, other), jnp.where(low, other, x)


def block_kappa(kappa, t):
    block = lanes((1, 128)) // 8
    out = jnp.zeros((1, 128), F32)
    for j in range(4):
        for c in range(2):
            if 4 * t + j < 9:
                out = jnp.where((block % 4 == j) & (block // 8 == c), kappa[4 * t + j + 9 * c], out)
    return out


def block_sources(tiles, scale):
    shape = tiles[0].shape
    block = lanes(shape) // 8
    low, j = block < 8, block % 4
    ng = spread(tiles[2], 2)
    nucl, grow = jnp.where(low, ng, 0.0), jnp.where(low, roll(ng, 64), 0.0)
    y = spread(tiles[1], 2)
    birth = nucl * y * y
    sink = jnp.where(low, (0.3 * scale) * spread(tiles[0], 0), 0.0)
    before = (roll(tiles[0], 8), jnp.where(j == 0, roll(tiles[0], -24), roll(tiles[1], 8)))
    out = []
    for t in range(2):
        order = (scale / 3.0) * (j + 4 * t).astype(F32)
        out.append((0.5 * scale) * birth + (order * grow) * before[t] - sink * tiles[t])
    out[1] = jnp.where(j < 2, out[1], jnp.where(j == 2, (-0.2 * scale) * birth, 0.0))
    return out


def unpack(tile, b):
    lane = lanes(tile.shape)
    return jnp.where((lane < 4) | (lane >= 124), roll(tile, 124 - 8 * b), 0.0)


def sources(get, nucl, grow, scale):
    y = get(6)
    birth = nucl * y * y
    moms = [get(k) for k in range(6)]
    half = (0.5 * scale) * birth
    sink = (0.3 * scale) * moms[0]
    out = []
    for k in range(6):
        s = half - sink * moms[k]
        if k:
            s = s + ((scale * k / 3.0) * grow) * moms[k - 1]
        out.append(s)
    return out + [(-0.2 * scale) * birth]


def planes(p):
    for slot in range(4):
        field, ny = p + 9 * (slot // 2), slot % 2
        yield 2 * field + ny, field, ny, p // 4, 4 * slot + p % 4


def across(kq, g):
    return jnp.concatenate([*split(kq), *split(g)], axis=1)


def down_rows(kq, f):
    return jnp.concatenate([*split(kq), *split(f)], axis=0)


GROUP = 3


def groups(fn):
    def step(i, _):
        for k in range(GROUP):
            fn(i * GROUP + k)
        return _

    lax.fori_loop(0, 9 // GROUP, step, 0)


def plane_velocities(fields, us, ws, scale):
    for ny in range(2):
        us[ny] = fields[36 + ny] * (scale / first_part)
        ws[ny] = fields[38 + ny] * (scale / first_part)


def first_stage(kappa, fields, a_rows, z_main, part, us, ws):
    dt = time_step
    plane_velocities(fields, us, ws, dt)

    def one(p):
        lhs, rhs = [], []
        for i, field, ny, t, b in planes(p):
            v = fields[i]
            kq = (kappa[field] * (dt / second_part)) * v
            lhs.append(across(kq, ws[ny] * v))
            rhs.append(down_rows(kq, us[ny] * v))
        z = dot(jnp.concatenate(lhs, axis=0), z_main[...])
        x = [dot(a_rows[...], jnp.concatenate(rhs[c : c + 2], axis=1)) for c in (0, 2)]
        for n, (i, field, ny, t, b) in enumerate(planes(p)):
            part[i] = fields[i] + z[64 * n : 64 * n + 64] + x[n // 2][:, 128 * ny : 128 * ny + 128]

    groups(one)
    for ny in range(2):
        src = sources(lambda k: fields[2 * k + ny], fields[40 + ny], fields[42 + ny], dt)
        for k in range(7):
            part[2 * k + ny] += src[k]


def interior(
    kappa, fields, part, z_near, z_far, near, far, a_rows, z_main, z_outer, z_inner, q1, pq1, pws, half,
    us, ws, el, cor,
):
    dt, scale = time_step, 0.5 * time_step
    kap = [block_kappa(kappa, t) for t in range(3)]
    from_left, from_right, to_left, to_right = [], [], [], []
    for t in range(3):
        for pair, one, two in ((sides(near[t], far[t]), from_left, from_right), (sides(z_near[t], z_far[t]), to_left, to_right)):
            one.append(pair[0])
            two.append(pair[1])
    pus, rhs, outer = [], [], []
    for n, side in enumerate((from_left, to_left, from_right, to_right)):
        u, w = block_velocity(side[2])
        w = w * (dt / first_part)
        if n % 2 == 0:
            pus.append(u * (dt / first_part))
            rhs.append(w)
        for t in range(3):
            kq = (kap[t] * (dt / second_part)) * side[t]
            el[64 * t : 64 * t + 64, 512 * n : 512 * n + 512] = across(kq, w * side[t])
    z = dot(el[...], z_outer[...])
    u, w = outer_tile(*pus), outer_tile(*rhs)
    pws[...] = w
    outer = [outer_tile(from_left[t], from_right[t]) for t in range(3)]
    rhs = []
    for t in range(3):
        kq = (kap[t] * (dt / second_part)) * outer[t]
        el[64 * t : 64 * t + 64, 0:512] = across(kq, w * outer[t])
        rhs.append(down_rows(kq, u * outer[t]))
    cor[...] = dot(el[:, 0:512], z_inner[...])
    x = dot(a_rows[...], jnp.concatenate(rhs, axis=1))
    for t in range(3):
        pq1[t] = outer[t] + x[:, 128 * t : 128 * t + 128] + z[64 * t : 64 * t + 64]
    for t, src in enumerate(block_sources(outer, dt)):
        pq1[t] += src
    for p in range(9):
        for i, field, ny, t, b in planes(p):
            q1[i] = part[i] + unpack(cor[64 * t : 64 * t + 64, :], b)

    plane_velocities(fields, us, ws, scale)
    for t in range(3):
        e = pq1[t, 8:56, :]
        el[48 * t : 48 * t + 48, 0:512] = across((kap[t] * (scale / second_part)) * e, (0.5 * pws[8:56, :]) * e)
    cor[0:144, :] = dot(el[0:144, 0:512], z_inner[...])

    def two(p):
        lhs, rhs = [], []
        for i, field, ny, t, b in planes(p):
            v = q1[i]
            kq = (kappa[field] * (scale / second_part)) * v
            mid = v[8:56]
            lhs.append(across(kq[8:56], ws[ny, 8:56, :] * mid))
            rhs.append(down_rows(kq, us[ny] * v))
        z = dot(jnp.concatenate(lhs, axis=0), z_main[...])
        x = [dot(a_rows[8:56, :], jnp.concatenate(rhs[c : c + 2], axis=1)) for c in (0, 2)]
        for n, (i, field, ny, t, b) in enumerate(planes(p)):
            half[i, 8:56, :] = (
                0.5 * (fields[i, 8:56, :] + q1[i, 8:56, :])
                + z[48 * n : 48 * n + 48]
                + x[n // 2][:, 128 * ny : 128 * ny + 128]
                + unpack(cor[48 * t : 48 * t + 48, :], b)
            )

    for p in range(9):
        two(p)
    for ny in range(2):
        src = sources(
            lambda k: q1[2 * k + ny, 8:56, :], fields[40 + ny, 8:56, :], fields[42 + ny, 8:56, :], scale
        )
        for k in range(7):
            half[2 * k + ny, 8:56, :] += src[k]


def edges(
    kappa, fields, q1, pq1, pws, half, first, second, first_corner, second_corner,
    a_one, a_two, a_corner, z_main, z_inner, out_mom, out_sca,
    s1h, s1a, lz, done, sems,
):
    outs = [(out_mom, 0, 12), (out_sca, 12, 24)]
    copies = [
        pltpu.make_async_copy(
            half.at[pl.ds(at, size), pl.ds(8, 48)], out.at[pl.ds(0, size), pl.ds(8, 48)], sems.at[n]
        )
        for n, (out, at, size) in enumerate(outs)
    ]
    for copy in copies:
        copy.start()
    dt, scale = time_step, 0.5 * time_step
    one, two = dt / first_part, scale / first_part
    front = lax.broadcasted_iota(jnp.int32, (8, 128), 0) < 4
    below_first = halves(1 - odd_of("gx"))
    pair = lambda *tiles: jnp.concatenate(tiles, axis=0)
    at_h = lambda a, b, i: jnp.where(below_first, a[i], b[i])
    at_o = lambda a, b, i: jnp.where(below_first, b[i], a[i])
    at_a = lambda ref, *i: jnp.where(front, ref[*i, 0:8, :], ref[*i, 56:64, :])
    at_b = lambda ref, *i: jnp.where(front, ref[*i, 56:64, :], ref[*i, 0:8, :])
    at_c = lambda ref, *i: jnp.where(front, ref[*i, 8:16, :], ref[*i, 48:56, :])
    other_h = lambda a, b, i: pltpu.roll(at_o(a, b, i), 4, 0)

    uh = [at_h(first, second, 36 + ny) for ny in range(2)]
    uo = [at_o(first, second, 36 + ny) for ny in range(2)]
    wh = [at_h(first, second, 38) * one, other_h(first, second, 38) * one]
    ua = [at_a(fields, 36 + ny) for ny in range(2)]
    u_ho = [pair(uh[ny], uo[ny]) * one for ny in range(2)]
    u_hc = [pair(uh[ny], at_c(fields, 36 + ny)) * two for ny in range(2)]
    u_ab = [pair(ua[ny], at_b(fields, 36 + ny)) * two for ny in range(2)]
    w_ab = [pair(at_a(fields, 38 + ny), at_b(fields, 38 + ny)) * two for ny in range(2)]

    kap = [block_kappa(kappa, t) for t in range(3)]
    outer = [
        at_h(first_corner, second_corner, 0),
        other_h(first_corner, second_corner, 0),
        at_h(first_corner, second_corner, 1),
    ]
    u, w = block_velocity(outer[2])
    u, w = u * one, w * one
    rhs, kqs, gs = [], [], []
    for t in range(3):
        kq = (kap[t] * (dt / second_part)) * outer[t]
        rhs.append(pair(*split(pair(kq, u * outer[t]))))
        kqs.append(kq)
        gs.append(w * outer[t])
    zero = jnp.zeros((8, 128), F32)
    cor_h = dot(across(pair(*kqs, zero), pair(*gs, zero)), z_inner[...])
    x = dot(a_corner[...], jnp.concatenate(rhs, axis=1))
    lhs = []
    for t in range(3):
        e = pair(at_a(pq1, t) + x[0:8, 128 * t : 128 * t + 128], at_b(pq1, t))
        w = pair(at_a(pws), at_b(pws)) * 0.5
        lhs.append(across((kap[t] * (scale / second_part)) * e, w * e))
    cor_ab = dot(pair(*lhs), z_inner[...])

    hs = lambda i: at_h(first, second, i)
    for field in range(18):
        k = kappa[field] * (dt / second_part)
        h = [hs(2 * field + ny) for ny in range(2)]
        lz[16 * field : 16 * field + 16, :] = across(pair(k * h[0], k * h[1]), pair(wh[0] * h[0], wh[1] * h[1]))
    z = dot(lz[...], z_main[...])
    for p in range(9):
        rhs = []
        for i, field, ny, t, b in planes(p):
            k = kappa[field] * (dt / second_part)
            ho, a = pair(hs(i), at_o(first, second, i)), at_a(fields, i)
            rhs.append(down_rows(k * ho, u_ho[ny] * ho))
            rhs[-1] = pair(rhs[-1], *split(pair(k * a, (ua[ny] * one) * a)))
        x = dot(a_one[...], jnp.concatenate(rhs, axis=1))
        for n, (i, field, ny, t, b) in enumerate(planes(p)):
            at = 16 * field + 8 * ny
            x_i = x[:, 128 * n : 128 * n + 128]
            s1h[i] = hs(i) + x_i[0:8] + z[at : at + 8] + unpack(cor_h[8 * t : 8 * t + 8], b)
            s1a[i] = at_a(q1, i) + x_i[8:16]
    for ny in range(2):
        src = sources(
            lambda k: hs(2 * k + ny), at_h(first, second, 39 + ny), other_h(first, second, 39 + ny), dt
        )
        for k in range(7):
            s1h[2 * k + ny] += src[k]

    for p in range(9):
        lhs, rhs = [], []
        for i, field, ny, t, b in planes(p):
            k = kappa[field] * (scale / second_part)
            ab, hc = pair(s1a[i], at_b(q1, i)), pair(s1h[i], at_c(q1, i))
            kq = split(k * ab)
            lhs.append(jnp.concatenate([*kq, *split(w_ab[ny] * ab)], axis=1))
            rhs.append(pair(*kq, *split(u_ab[ny] * ab), down_rows(k * hc, u_hc[ny] * hc)))
        z = dot(pair(*lhs), z_main[...])
        x = dot(a_two[...], jnp.concatenate(rhs, axis=1))
        for n, (i, field, ny, t, b) in enumerate(planes(p)):
            own = pair(at_a(fields, i) + s1a[i], at_b(fields, i) + at_b(q1, i))
            done[i] = (
                0.5 * own
                + z[16 * n : 16 * n + 16]
                + x[:, 128 * n : 128 * n + 128]
                + unpack(cor_ab[16 * t : 16 * t + 16], b)
            )
    for ny in range(2):
        nucl = pair(at_a(fields, 40 + ny), at_b(fields, 40 + ny))
        grow = pair(at_a(fields, 42 + ny), at_b(fields, 42 + ny))
        src = sources(lambda k: pair(s1a[2 * k + ny], at_b(q1, 2 * k + ny)), nucl, grow, scale)
        for k in range(7):
            done[2 * k + ny] += src[k]
    for i in range(36):
        a, b = done[i, 0:8, :], done[i, 8:16, :]
        done[i, 0:8, :] = jnp.where(front, a, b)
        done[i, 8:16, :] = jnp.where(front, b, a)
    last = [
        pltpu.make_async_copy(
            done.at[pl.ds(at, size), pl.ds(8 * side, 8)],
            out.at[pl.ds(0, size), pl.ds(56 * side, 8)],
            sems.at[2 + 2 * n + side],
        )
        for n, (out, at, size) in enumerate(outs)
        for side in range(2)
    ]
    for copy in last:
        copy.start()
    for copy in copies + last:
        copy.wait()


def call(kernel, outs, cost, mib=24, **kw):
    return pl.pallas_call(
        kernel,
        out_shape=[jax.ShapeDtypeStruct(o, F32) for o in outs],
        cost_estimate=pl.CostEstimate(flops=cost, bytes_accessed=cost // 4, transcendentals=0),
        compiler_params=pltpu.CompilerParams(vmem_limit_bytes=mib * 2**20),
        **kw,
    )


def swap(value, axis, far):
    peers = lax.axis_size(axis)
    other = lambda i: (((i + far) ^ 1) - far) % peers
    return lax.ppermute(value, axis, [(i, other(i)) for i in range(peers)])


def body(moments, scalars, velocity, diffusivity, nucleation, growth):
    vmem = pl.BlockSpec(memory_space=pltpu.VMEM)
    smem = pl.BlockSpec(memory_space=pltpu.SMEM)
    hbm = pl.BlockSpec(memory_space=pltpu.HBM)
    tiles = lambda *lead: pltpu.VMEM(lead + (128,), F32)
    flat = [
        pltpu.with_memory_space_constraint(x.reshape(-1, 64, 128), pltpu.HBM)
        for x in (moments, scalars, velocity, nucleation, growth)
    ]
    a_rows, a_one, a_two, a_corner, z_main, z_outer, z_inner = (jnp.asarray(m) for m in matrices())

    z_far, z_near, fields = call(
        pack_z,
        [(3, 64, 128), (3, 64, 128), (44, 64, 128)],
        10**6,
        in_specs=[hbm] * 5,
        out_specs=[vmem] * 3,
        scratch_shapes=[pltpu.SemaphoreType.DMA((10,))],
    )(*flat)
    far = swap(z_far, "gz", 1)
    x_first, x_second, z_near = call(x_messages, [(41, 8, 128), (41, 8, 128), (3, 64, 128)], 10**5)(fields, z_near)
    near = swap(z_near, "gz", 0)
    (part,) = call(
        first_stage,
        [(36, 64, 128)],
        10**7,
        in_specs=[smem] + [vmem] * 3,
        scratch_shapes=[tiles(2, 64), tiles(2, 64)],
    )(diffusivity, fields, a_rows, z_main)
    second = swap(x_second, "gx", 1)
    first = swap(x_first, "gx", 0)
    c_first, c_second = call(corners, [(2, 8, 128)] * 2, 10**6)(near, far, part)
    second_corner = swap(c_second, "gx", 1)
    first_corner = swap(c_first, "gx", 0)
    q1, pq1, pws, half = call(
        interior,
        [(36, 64, 128), (3, 64, 128), (64, 128), (36, 64, 128)],
        10 * 10**8,
        in_specs=[smem] + [vmem] * 10,
        scratch_shapes=[tiles(2, 64), tiles(2, 64), pltpu.VMEM((192, 2048), BF16), tiles(192)],
    )(diffusivity, fields, part, z_near, z_far, near, far, a_rows, z_main, z_outer, z_inner)
    out_mom, out_sca = call(
        edges,
        [(12, 64, 128), (24, 64, 128)],
        10**8,
        in_specs=[smem] + [vmem] * 14,
        out_specs=[hbm] * 2,
        scratch_shapes=[
            tiles(36, 8), tiles(36, 8), pltpu.VMEM((288, 512), BF16), tiles(36, 16), pltpu.SemaphoreType.DMA((6,)),
        ],
    )(
        diffusivity, fields, q1, pq1, pws, half, first, second, first_corner, second_corner,
        a_one, a_two, a_corner, z_main, z_inner,
    )
    return out_mom.reshape(moments.shape), out_sca.reshape(scalars.shape)


def solution(mesh):
    return jax.shard_map(
        body,
        mesh=mesh,
        in_specs=(
            P(None, None, "gx", "gz"),
            P(None, None, "gx", "gz"),
            P(None, None, "gx", "gz"),
            P(),
            P(None, "gx", "gz"),
            P(None, "gx", "gz"),
        ),
        out_specs=(P(None, None, "gx", "gz"), P(None, None, "gx", "gz")),
        check_vma=False,
    )
```

```python
import numpy as np

import jax
import jax.numpy as jnp
from jax import lax
from jax.experimental import pallas as pl
from jax.experimental.pallas import tpu as pltpu
from jax.sharding import PartitionSpec as P

first_whole, first_part = (672.0, -168.0, 32.0, -3.0), 840.0
second_whole, second_part = (8064.0, -1008.0, 128.0, -9.0), 5040.0
centre_x, centre_z = -28672.0, -28.0
time_step = 0.25

F32, BF16 = jnp.float32, jnp.bfloat16


def band(targets, sources, centre):
    gap = np.asarray(sources)[None, :] - np.asarray(targets)[:, None]
    second = np.where(gap == 0, centre, 0.0)
    first = np.zeros(gap.shape)
    for m in range(1, 5):
        second = second + second_whole[m - 1] * (abs(gap) == m)
        first = first - first_whole[m - 1] * ((gap == m) * 1.0 - (gap == -m))
    return second, first


rows_h = [64, 65, 66, 67, -4, -3, -2, -1]
rows_o = [-8, -7, -6, -5, 68, 69, 70, 71]
rows_a = [0, 1, 2, 3, 60, 61, 62, 63]
rows_b = [56, 57, 58, 59, 4, 5, 6, 7]
rows_c = [8, 9, 10, 11, 52, 53, 54, 55]


def matrices():
    both = lambda pair, axis: np.concatenate([pair[0], pair[0], pair[1], pair[1]], axis=axis)
    rows, cols = np.arange(64), np.arange(128)
    a_rows = both(band(rows, rows, centre_x), 1)
    far = band(rows_h + rows_a, rows_h + rows_o, centre_x)
    own = [m * (np.arange(16) < 8)[:, None] for m in band(rows_h + rows_a, rows_a, centre_x)]
    a_one = np.concatenate([both(far, 1), own[0], own[1], own[0], own[1]], axis=1)
    a_two = np.concatenate(
        [both(band(rows_a + rows_b, src, centre_x), 1) for src in (rows_a + rows_b, rows_h + rows_c)], axis=1
    )
    corner = [np.concatenate([m, 0 * m]) for m in band(rows_a, rows_h, centre_x)]
    a_corner = np.concatenate(corner + corner, axis=1)
    z_main = both([m.T for m in band(cols, cols, centre_z)], 0)
    blocks = lambda pair: both([np.kron(np.eye(16), m.T) for m in pair], 0)
    outer = [128, 129, 130, 131, -4, -3, -2, -1]
    z_outer = np.concatenate(
        [blocks(band(outer, np.arange(at, at + 8), centre_z)) for at in (-8, 0, 128, 120)]
    )
    z_inner = blocks(band([124, 125, 126, 127, 0, 1, 2, 3], outer, centre_z))
    return [m.astype(BF16) for m in (a_rows, a_one, a_two, a_corner, z_main, z_outer, z_inner)]


def lanes(shape=(8, 128)):
    return lax.broadcasted_iota(jnp.int32, shape, len(shape) - 1)


def roll(x, by):
    by = by % 128
    return x if by == 0 else pltpu.roll(x, by, 1)


def split(x):
    high = x.astype(BF16)
    return high, (x - high.astype(F32)).astype(BF16)


def dot(a, b):
    return jnp.dot(a, b, preferred_element_type=F32)


def plane_of(p, s):
    c, ny = s // 2, s % 2
    return 2 * (p + 9 * c) + ny if p < 9 else 4 * p + s


def odd_of(axis):
    return lax.axis_index(axis) % 2


def z_messages(fields, r, t):
    pair, odd = lanes() // 16, (lanes() // 8) % 2 == 1
    tile = [None, None]
    for j in range(4 if t < 2 else 3):
        for s in range(4):
            c = 2 * s + j // 2
            one = roll(fields[plane_of(4 * t + j, s), r : r + 8, :], 16 * c + 8)
            half = tile[j % 2]
            tile[j % 2] = one if half is None else jnp.where(pair == c, one, half)
    return jnp.where(odd, tile[1], roll(tile[0], -8)), jnp.where(odd, roll(tile[1], 8), tile[0])


def pack_z(mom, sca, vel, nuc, gro, far, near, fields, sems):
    parts = [
        [(mom, 0, 0, 8), (sca, 6, 18, 8)],
        [(mom, 8, 8, 4), (sca, 0, 12, 4), (sca, 14, 26, 8)],
        [(sca, 4, 16, 2), (sca, 22, 34, 2), (vel, 0, 36, 4), (nuc, 0, 40, 2), (gro, 0, 42, 2)],
    ]
    copies, n = [], 0
    for part in parts:
        copies.append([])
        for src, at, to, size in part:
            copies[-1].append(
                pltpu.make_async_copy(src.at[pl.ds(at, size)], fields.at[pl.ds(to, size)], sems.at[n])
            )
            copies[-1][-1].start()
            n += 1
    right = odd_of("gz") == 0
    for t in range(3):
        for copy in copies[t]:
            copy.wait()
        for r in range(0, 64, 8):
            zl, zr = z_messages(fields, r, t)
            far[t, r : r + 8, :] = jnp.where(right, zl, zr)
            near[t, r : r + 8, :] = jnp.where(right, zr, zl)


def halves(first):
    return (lax.broadcasted_iota(jnp.int32, (8, 128), 0) + 4 * first) % 8 >= 4


def x_messages(fields, z_near, first, second, near):
    near[...] = z_near[...]
    odd = odd_of("gx") == 1
    for k, msg in enumerate((first, second)):
        low = odd if k == 0 else jnp.logical_not(odd)
        at = pl.ds(pl.multiple_of(jnp.where(low, 0, 56), 8), 8)
        for i in range(38):
            msg[i] = fields[i, at, :]
        keep = halves(low.astype(jnp.int32))
        for n, (i, j) in enumerate(((38, 39), (40, 42), (41, 43))):
            msg[38 + n] = jnp.where(keep, fields[i, at, :], pltpu.roll(fields[j, at, :], 4, 0))


def outer_tile(from_left, from_right):
    return jnp.where(lanes(from_left.shape) % 8 >= 4, from_left, from_right)


def sides(near, far):
    right = odd_of("gz") == 0
    return jnp.where(right, far, near), jnp.where(right, near, far)


def corners(near, far, part, first, second):
    del part
    odd = odd_of("gx") == 1
    for k, msg in enumerate((first, second)):
        low = odd if k == 0 else jnp.logical_not(odd)
        at = pl.ds(pl.multiple_of(jnp.where(low, 0, 56), 8), 8)
        keep = halves(low.astype(jnp.int32))
        tile = [outer_tile(*sides(near[t, at, :], far[t, at, :])) for t in range(3)]
        msg[0] = jnp.where(keep, tile[0], pltpu.roll(tile[1], 4, 0))
        msg[1] = jnp.where(keep, tile[2], 0.0)


def spread(tile, j):
    x = jnp.where((lanes(tile.shape) // 8) % 4 == j, tile, 0.0)
    x = x + roll(x, -8 if j % 2 else 8)
    return x + roll(x, -16 if j >= 2 else 16)


def block_velocity(tile):
    x = spread(tile, 1)
    low, other = lanes(tile.shape) < 64, roll(x, 64)
    return jnp.where(low, x, other), jnp.where(low, other, x)


def block_kappa(kappa, t):
    block = lanes((1, 128)) // 8
    out = jnp.zeros((1, 128), F32)
    for j in range(4):
        for c in range(2):
            if 4 * t + j < 9:
                out = jnp.where((block % 4 == j) & (block // 8 == c), kappa[4 * t + j + 9 * c], out)
    return out


def block_sources(tiles, scale):
    shape = tiles[0].shape
    block = lanes(shape) // 8
    low, j = block < 8, block % 4
    ng = spread(tiles[2], 2)
    nucl, grow = jnp.where(low, ng, 0.0), jnp.where(low, roll(ng, 64), 0.0)
    y = spread(tiles[1], 2)
    birth = nucl * y * y
    sink = jnp.where(low, (0.3 * scale) * spread(tiles[0], 0), 0.0)
    before = (roll(tiles[0], 8), jnp.where(j == 0, roll(tiles[0], -24), roll(tiles[1], 8)))
    out = []
    for t in range(2):
        order = (scale / 3.0) * (j + 4 * t).astype(F32)
        out.append((0.5 * scale) * birth + (order * grow) * before[t] - sink * tiles[t])
    out[1] = jnp.where(j < 2, out[1], jnp.where(j == 2, (-0.2 * scale) * birth, 0.0))
    return out


def unpack(tile, b):
    lane = lanes(tile.shape)
    return jnp.where((lane < 4) | (lane >= 124), roll(tile, 124 - 8 * b), 0.0)


def sources(get, nucl, grow, scale):
    y = get(6)
    birth = nucl * y * y
    moms = [get(k) for k in range(6)]
    half = (0.5 * scale) * birth
    sink = (0.3 * scale) * moms[0]
    out = []
    for k in range(6):
        s = half - sink * moms[k]
        if k:
            s = s + ((scale * k / 3.0) * grow) * moms[k - 1]
        out.append(s)
    return out + [(-0.2 * scale) * birth]


def planes(p):
    for slot in range(4):
        field, ny = p + 9 * (slot // 2), slot % 2
        yield 2 * field + ny, field, ny, p // 4, 4 * slot + p % 4


def across(kq, g):
    return jnp.concatenate([*split(kq), *split(g)], axis=1)


def down_rows(kq, f):
    return jnp.concatenate([*split(kq), *split(f)], axis=0)


GROUP = 3


def groups(fn):
    def step(i, _):
        for k in range(GROUP):
            fn(i * GROUP + k)
        return _

    lax.fori_loop(0, 9 // GROUP, step, 0)


def plane_velocities(fields, us, ws, scale):
    for ny in range(2):
        us[ny] = fields[36 + ny] * (scale / first_part)
        ws[ny] = fields[38 + ny] * (scale / first_part)


def first_stage(kappa, fields, a_rows, z_main, part, us, ws):
    dt = time_step
    plane_velocities(fields, us, ws, dt)

    def one(p):
        lhs, rhs = [], []
        for i, field, ny, t, b in planes(p):
            v = fields[i]
            kq = (kappa[field] * (dt / second_part)) * v
            lhs.append(across(kq, ws[ny] * v))
            rhs.append(down_rows(kq, us[ny] * v))
        z = dot(jnp.concatenate(lhs, axis=0), z_main[...])
        x = [dot(a_rows[...], jnp.concatenate(rhs[c : c + 2], axis=1)) for c in (0, 2)]
        for n, (i, field, ny, t, b) in enumerate(planes(p)):
            part[i] = fields[i] + z[64 * n : 64 * n + 64] + x[n // 2][:, 128 * ny : 128 * ny + 128]

    groups(one)
    for ny in range(2):
        src = sources(lambda k: fields[2 * k + ny], fields[40 + ny], fields[42 + ny], dt)
        for k in range(7):
            part[2 * k + ny] += src[k]


def interior(
    kappa, fields, part, z_near, z_far, near, far, a_rows, z_main, z_outer, z_inner, q1, pq1, pws, half,
    us, ws, el, cor,
):
    dt, scale = time_step, 0.5 * time_step
    kap = [block_kappa(kappa, t) for t in range(3)]
    from_left, from_right, to_left, to_right = [], [], [], []
    for t in range(3):
        for pair, one, two in ((sides(near[t], far[t]), from_left, from_right), (sides(z_near[t], z_far[t]), to_left, to_right)):
            one.append(pair[0])
            two.append(pair[1])
    pus, rhs, outer = [], [], []
    for n, side in enumerate((from_left, to_left, from_right, to_right)):
        u, w = block_velocity(side[2])
        w = w * (dt / first_part)
        if n % 2 == 0:
            pus.append(u * (dt / first_part))
            rhs.append(w)
        for t in range(3):
            kq = (kap[t] * (dt / second_part)) * side[t]
            el[64 * t : 64 * t + 64, 512 * n : 512 * n + 512] = across(kq, w * side[t])
    z = dot(el[...], z_outer[...])
    u, w = outer_tile(*pus), outer_tile(*rhs)
    pws[...] = w
    outer = [outer_tile(from_left[t], from_right[t]) for t in range(3)]
    rhs = []
    for t in range(3):
        kq = (kap[t] * (dt / second_part)) * outer[t]
        el[64 * t : 64 * t + 64, 0:512] = across(kq, w * outer[t])
        rhs.append(down_rows(kq, u * outer[t]))
    cor[...] = dot(el[:, 0:512], z_inner[...])
    x = dot(a_rows[...], jnp.concatenate(rhs, axis=1))
    for t in range(3):
        pq1[t] = outer[t] + x[:, 128 * t : 128 * t + 128] + z[64 * t : 64 * t + 64]
    for t, src in enumerate(block_sources(outer, dt)):
        pq1[t] += src
    for p in range(9):
        for i, field, ny, t, b in planes(p):
            q1[i] = part[i] + unpack(cor[64 * t : 64 * t + 64, :], b)

    plane_velocities(fields, us, ws, scale)
    for t in range(3):
        e = pq1[t, 8:56, :]
        el[48 * t : 48 * t + 48, 0:512] = across((kap[t] * (scale / second_part)) * e, (0.5 * pws[8:56, :]) * e)
    cor[0:144, :] = dot(el[0:144, 0:512], z_inner[...])

    def two(p):
        lhs, rhs = [], []
        for i, field, ny, t, b in planes(p):
            v = q1[i]
            kq = (kappa[field] * (scale / second_part)) * v
            mid = v[8:56]
            lhs.append(across(kq[8:56], ws[ny, 8:56, :] * mid))
            rhs.append(down_rows(kq, us[ny] * v))
        z = dot(jnp.concatenate(lhs, axis=0), z_main[...])
        x = [dot(a_rows[8:56, :], jnp.concatenate(rhs[c : c + 2], axis=1)) for c in (0, 2)]
        for n, (i, field, ny, t, b) in enumerate(planes(p)):
            half[i, 8:56, :] = (
                0.5 * (fields[i, 8:56, :] + q1[i, 8:56, :])
                + z[48 * n : 48 * n + 48]
                + x[n // 2][:, 128 * ny : 128 * ny + 128]
                + unpack(cor[48 * t : 48 * t + 48, :], b)
            )

    for p in range(9):
        two(p)
    for ny in range(2):
        src = sources(
            lambda k: q1[2 * k + ny, 8:56, :], fields[40 + ny, 8:56, :], fields[42 + ny, 8:56, :], scale
        )
        for k in range(7):
            half[2 * k + ny, 8:56, :] += src[k]


def edges(
    kappa, fields, q1, pq1, pws, half, first, second, second_corner, first_corner,
    a_one, a_two, a_corner, z_main, z_inner, out_mom, out_sca,
    s1h, s1a, lz, done, sems,
):
    outs = [(out_mom, 0, 12), (out_sca, 12, 24)]
    copies = [
        pltpu.make_async_copy(
            half.at[pl.ds(at, size), pl.ds(8, 48)], out.at[pl.ds(0, size), pl.ds(8, 48)], sems.at[n]
        )
        for n, (out, at, size) in enumerate(outs)
    ]
    for copy in copies:
        copy.start()
    dt, scale = time_step, 0.5 * time_step
    one, two = dt / first_part, scale / first_part
    front = lax.broadcasted_iota(jnp.int32, (8, 128), 0) < 4
    below_first = halves(1 - odd_of("gx"))
    pair = lambda *tiles: jnp.concatenate(tiles, axis=0)
    at_h = lambda a, b, i: jnp.where(below_first, a[i], b[i])
    at_o = lambda a, b, i: jnp.where(below_first, b[i], a[i])
    at_a = lambda ref, *i: jnp.where(front, ref[*i, 0:8, :], ref[*i, 56:64, :])
    at_b = lambda ref, *i: jnp.where(front, ref[*i, 56:64, :], ref[*i, 0:8, :])
    at_c = lambda ref, *i: jnp.where(front, ref[*i, 8:16, :], ref[*i, 48:56, :])
    other_h = lambda a, b, i: pltpu.roll(at_o(a, b, i), 4, 0)

    uh = [at_h(first, second, 36 + ny) for ny in range(2)]
    uo = [at_o(first, second, 36 + ny) for ny in range(2)]
    wh = [at_h(first, second, 38) * one, other_h(first, second, 38) * one]
    ua = [at_a(fields, 36 + ny) for ny in range(2)]
    u_ho = [pair(uh[ny], uo[ny]) * one for ny in range(2)]
    u_hc = [pair(uh[ny], at_c(fields, 36 + ny)) * two for ny in range(2)]
    u_ab = [pair(ua[ny], at_b(fields, 36 + ny)) * two for ny in range(2)]
    w_ab = [pair(at_a(fields, 38 + ny), at_b(fields, 38 + ny)) * two for ny in range(2)]

    kap = [block_kappa(kappa, t) for t in range(3)]
    outer = [
        at_h(first_corner, second_corner, 0),
        other_h(first_corner, second_corner, 0),
        at_h(first_corner, second_corner, 1),
    ]
    u, w = block_velocity(outer[2])
    u, w = u * one, w * one
    rhs, kqs, gs = [], [], []
    for t in range(3):
        kq = (kap[t] * (dt / second_part)) * outer[t]
        rhs.append(pair(*split(pair(kq, u * outer[t]))))
        kqs.append(kq)
        gs.append(w * outer[t])
    zero = jnp.zeros((8, 128), F32)
    cor_h = dot(across(pair(*kqs, zero), pair(*gs, zero)), z_inner[...])
    x = dot(a_corner[...], jnp.concatenate(rhs, axis=1))
    lhs = []
    for t in range(3):
        e = pair(at_a(pq1, t) + x[0:8, 128 * t : 128 * t + 128], at_b(pq1, t))
        w = pair(at_a(pws), at_b(pws)) * 0.5
        lhs.append(across((kap[t] * (scale / second_part)) * e, w * e))
    cor_ab = dot(pair(*lhs), z_inner[...])

    hs = lambda i: at_h(first, second, i)
    for field in range(18):
        k = kappa[field] * (dt / second_part)
        h = [hs(2 * field + ny) for ny in range(2)]
        lz[16 * field : 16 * field + 16, :] = across(pair(k * h[0], k * h[1]), pair(wh[0] * h[0], wh[1] * h[1]))
    z = dot(lz[...], z_main[...])
    for p in range(9):
        rhs = []
        for i, field, ny, t, b in planes(p):
            k = kappa[field] * (dt / second_part)
            ho, a = pair(hs(i), at_o(first, second, i)), at_a(fields, i)
            rhs.append(down_rows(k * ho, u_ho[ny] * ho))
            rhs[-1] = pair(rhs[-1], *split(pair(k * a, (ua[ny] * one) * a)))
        x = dot(a_one[...], jnp.concatenate(rhs, axis=1))
        for n, (i, field, ny, t, b) in enumerate(planes(p)):
            at = 16 * field + 8 * ny
            x_i = x[:, 128 * n : 128 * n + 128]
            s1h[i] = hs(i) + x_i[0:8] + z[at : at + 8] + unpack(cor_h[8 * t : 8 * t + 8], b)
            s1a[i] = at_a(q1, i) + x_i[8:16]
    for ny in range(2):
        src = sources(
            lambda k: hs(2 * k + ny), at_h(first, second, 39 + ny), other_h(first, second, 39 + ny), dt
        )
        for k in range(7):
            s1h[2 * k + ny] += src[k]

    last = [
        pltpu.make_async_copy(
            done.at[pl.ds(at, size), pl.ds(8 * side, 8)],
            out.at[pl.ds(0, size), pl.ds(56 * side, 8)],
            sems.at[2 + 2 * n + side],
        )
        for n, (out, at, size) in enumerate(outs)
        for side in range(2)
    ]
    src = []
    for ny in range(2):
        nucl = pair(at_a(fields, 40 + ny), at_b(fields, 40 + ny))
        grow = pair(at_a(fields, 42 + ny), at_b(fields, 42 + ny))
        src.append(sources(lambda k: pair(s1a[2 * k + ny], at_b(q1, 2 * k + ny)), nucl, grow, scale))
    for p in range(9):
        if p == 6:
            for copy in last[:2]:
                copy.start()
        lhs, rhs = [], []
        for i, field, ny, t, b in planes(p):
            k = kappa[field] * (scale / second_part)
            ab, hc = pair(s1a[i], at_b(q1, i)), pair(s1h[i], at_c(q1, i))
            kq = split(k * ab)
            lhs.append(jnp.concatenate([*kq, *split(w_ab[ny] * ab)], axis=1))
            rhs.append(pair(*kq, *split(u_ab[ny] * ab), down_rows(k * hc, u_hc[ny] * hc)))
        z = dot(pair(*lhs), z_main[...])
        x = dot(a_two[...], jnp.concatenate(rhs, axis=1))
        for n, (i, field, ny, t, b) in enumerate(planes(p)):
            own = pair(at_a(fields, i) + s1a[i], at_b(fields, i) + at_b(q1, i))
            new = (
                0.5 * own
                + z[16 * n : 16 * n + 16]
                + x[:, 128 * n : 128 * n + 128]
                + unpack(cor_ab[16 * t : 16 * t + 16], b)
            )
            if field < 7:
                new = new + src[ny][field]
            done[i, 0:8, :] = jnp.where(front, new[0:8], new[8:16])
            done[i, 8:16, :] = jnp.where(front, new[8:16], new[0:8])
    for copy in last[2:]:
        copy.start()
    for copy in copies + last:
        copy.wait()


def call(kernel, outs, cost, mib=24, **kw):
    return pl.pallas_call(
        kernel,
        out_shape=[jax.ShapeDtypeStruct(o, F32) for o in outs],
        cost_estimate=pl.CostEstimate(flops=cost, bytes_accessed=cost // 4, transcendentals=0),
        compiler_params=pltpu.CompilerParams(vmem_limit_bytes=mib * 2**20),
        **kw,
    )


def swap(value, axis, far):
    peers = lax.axis_size(axis)
    other = lambda i: (((i + far) ^ 1) - far) % peers
    return lax.ppermute(value, axis, [(i, other(i)) for i in range(peers)])


def body(moments, scalars, velocity, diffusivity, nucleation, growth):
    vmem = pl.BlockSpec(memory_space=pltpu.VMEM)
    smem = pl.BlockSpec(memory_space=pltpu.SMEM)
    hbm = pl.BlockSpec(memory_space=pltpu.HBM)
    tiles = lambda *lead: pltpu.VMEM(lead + (128,), F32)
    flat = [
        pltpu.with_memory_space_constraint(x.reshape(-1, 64, 128), pltpu.HBM)
        for x in (moments, scalars, velocity, nucleation, growth)
    ]
    a_rows, a_one, a_two, a_corner, z_main, z_outer, z_inner = (jnp.asarray(m) for m in matrices())

    z_far, z_near, fields = call(
        pack_z,
        [(3, 64, 128), (3, 64, 128), (44, 64, 128)],
        10**6,
        in_specs=[hbm] * 5,
        out_specs=[vmem] * 3,
        scratch_shapes=[pltpu.SemaphoreType.DMA((10,))],
    )(*flat)
    far = swap(z_far, "gz", 1)
    x_first, x_second, z_near = call(x_messages, [(41, 8, 128), (41, 8, 128), (3, 64, 128)], 10**5)(fields, z_near)
    near = swap(z_near, "gz", 0)
    (part,) = call(
        first_stage,
        [(36, 64, 128)],
        10**7,
        in_specs=[smem] + [vmem] * 3,
        scratch_shapes=[tiles(2, 64), tiles(2, 64)],
    )(diffusivity, fields, a_rows, z_main)
    second = swap(x_second, "gx", 1)
    first = swap(x_first, "gx", 0)
    c_first, c_second = call(corners, [(2, 8, 128)] * 2, 10**6)(near, far, part)
    second_corner = swap(c_second, "gx", 1)
    first_corner = swap(c_first, "gx", 0)
    q1, pq1, pws, half = call(
        interior,
        [(36, 64, 128), (3, 64, 128), (64, 128), (36, 64, 128)],
        10 * 10**8,
        in_specs=[smem] + [vmem] * 10,
        scratch_shapes=[tiles(2, 64), tiles(2, 64), pltpu.VMEM((192, 2048), BF16), tiles(192)],
    )(diffusivity, fields, part, z_near, z_far, near, far, a_rows, z_main, z_outer, z_inner)
    out_mom, out_sca = call(
        edges,
        [(12, 64, 128), (24, 64, 128)],
        10**8,
        in_specs=[smem] + [vmem] * 14,
        out_specs=[hbm] * 2,
        scratch_shapes=[
            tiles(36, 8), tiles(36, 8), pltpu.VMEM((288, 512), BF16), tiles(36, 16), pltpu.SemaphoreType.DMA((6,)),
        ],
    )(
        diffusivity, fields, q1, pq1, pws, half, first, second, second_corner, first_corner,
        a_one, a_two, a_corner, z_main, z_inner,
    )
    return out_mom.reshape(moments.shape), out_sca.reshape(scalars.shape)


def solution(mesh):
    return jax.shard_map(
        body,
        mesh=mesh,
        in_specs=(
            P(None, None, "gx", "gz"),
            P(None, None, "gx", "gz"),
            P(None, None, "gx", "gz"),
            P(),
            P(None, "gx", "gz"),
            P(None, "gx", "gz"),
        ),
        out_specs=(P(None, None, "gx", "gz"), P(None, None, "gx", "gz")),
        check_vma=False,
    )
```

```python
import numpy as np

import jax
import jax.numpy as jnp
from jax import lax
from jax.experimental import pallas as pl
from jax.experimental.pallas import tpu as pltpu
from jax.sharding import PartitionSpec as P

first_whole, first_part = (672.0, -168.0, 32.0, -3.0), 840.0
second_whole, second_part = (8064.0, -1008.0, 128.0, -9.0), 5040.0
centre_x, centre_z = -28672.0, -28.0
time_step = 0.25

F32, BF16 = jnp.float32, jnp.bfloat16


def band(targets, sources, centre):
    gap = np.asarray(sources)[None, :] - np.asarray(targets)[:, None]
    second = np.where(gap == 0, centre, 0.0)
    first = np.zeros(gap.shape)
    for m in range(1, 5):
        second = second + second_whole[m - 1] * (abs(gap) == m)
        first = first - first_whole[m - 1] * ((gap == m) * 1.0 - (gap == -m))
    return second, first


rows_h = [64, 65, 66, 67, -4, -3, -2, -1]
rows_o = [-8, -7, -6, -5, 68, 69, 70, 71]
rows_a = [0, 1, 2, 3, 60, 61, 62, 63]
rows_b = [56, 57, 58, 59, 4, 5, 6, 7]
rows_c = [8, 9, 10, 11, 52, 53, 54, 55]


def matrices():
    both = lambda pair, axis: np.concatenate([pair[0], pair[0], pair[1], pair[1]], axis=axis)
    rows, cols = np.arange(64), np.arange(128)
    a_rows = both(band(rows, rows, centre_x), 1)
    far = band(rows_h + rows_a, rows_h + rows_o, centre_x)
    own = [m * (np.arange(16) < 8)[:, None] for m in band(rows_h + rows_a, rows_a, centre_x)]
    a_one = np.concatenate([both(far, 1), own[0], own[1], own[0], own[1]], axis=1)
    a_two = np.concatenate(
        [both(band(rows_a + rows_b, src, centre_x), 1) for src in (rows_a + rows_b, rows_h + rows_c)], axis=1
    )
    corner = [np.concatenate([m, 0 * m]) for m in band(rows_a, rows_h, centre_x)]
    a_corner = np.concatenate(corner + corner, axis=1)
    z_main = both([m.T for m in band(cols, cols, centre_z)], 0)
    blocks = lambda pair: both([np.kron(np.eye(16), m.T) for m in pair], 0)
    outer = [128, 129, 130, 131, -4, -3, -2, -1]
    z_outer = np.concatenate(
        [blocks(band(outer, np.arange(at, at + 8), centre_z)) for at in (-8, 0, 128, 120)]
    )
    z_inner = blocks(band([124, 125, 126, 127, 0, 1, 2, 3], outer, centre_z))
    return [m.astype(BF16) for m in (a_rows, a_one, a_two, a_corner, z_main, z_outer, z_inner)]


def lanes(shape=(8, 128)):
    return lax.broadcasted_iota(jnp.int32, shape, len(shape) - 1)


def roll(x, by):
    by = by % 128
    return x if by == 0 else pltpu.roll(x, by, 1)


def split(x):
    high = x.astype(BF16)
    return high, (x - high.astype(F32)).astype(BF16)


def dot(a, b):
    return jnp.dot(a, b, preferred_element_type=F32)


def plane_of(p, s):
    c, ny = s // 2, s % 2
    return 2 * (p + 9 * c) + ny if p < 9 else 4 * p + s


def odd_of(axis):
    return lax.axis_index(axis) % 2


def z_tiles(fields, r, t):
    pair = lanes() // 16
    tile = [None, None]
    for j in range(4 if t < 2 else 3):
        for s in range(4):
            c = 2 * s + j // 2
            one = roll(fields[plane_of(4 * t + j, s), r : r + 8, :], 16 * c + 8)
            half = tile[j % 2]
            tile[j % 2] = one if half is None else jnp.where(pair == c, one, half)
    return tile


def pack_z(mom, sca, vel, nuc, gro, far, near, fields, sems):
    parts = [
        [(mom, 0, 0, 8), (sca, 6, 18, 8)],
        [(mom, 8, 8, 4), (sca, 0, 12, 4), (sca, 14, 26, 8)],
        [(sca, 4, 16, 2), (sca, 22, 34, 2), (vel, 0, 36, 4), (nuc, 0, 40, 2), (gro, 0, 42, 2)],
    ]
    copies, n = [], 0
    for part in parts:
        copies.append([])
        for src, at, to, size in part:
            copies[-1].append(
                pltpu.make_async_copy(src.at[pl.ds(at, size)], fields.at[pl.ds(to, size)], sems.at[n])
            )
            copies[-1][-1].start()
            n += 1
    right = odd_of("gz") == 0
    odd = (lanes() // 8) % 2 == 1
    for t in range(3):
        for copy in copies[t]:
            copy.wait()
        made = [z_tiles(fields, r, t) for r in range(0, 64, 8)]
        for n, (one, two) in enumerate(made):
            zl, zr = jnp.where(odd, two, roll(one, -8)), jnp.where(odd, roll(two, 8), one)
            far[t, 8 * n : 8 * n + 8, :] = jnp.where(right, zl, zr)
            near[t, 8 * n : 8 * n + 8, :] = jnp.where(right, zr, zl)


def halves(first):
    return (lax.broadcasted_iota(jnp.int32, (8, 128), 0) + 4 * first) % 8 >= 4


def x_messages(fields, z_near, first, second, near):
    near[...] = z_near[...]
    odd = odd_of("gx") == 1
    for k, msg in enumerate((first, second)):
        low = odd if k == 0 else jnp.logical_not(odd)
        at = pl.ds(pl.multiple_of(jnp.where(low, 0, 56), 8), 8)
        for i in range(36):
            msg[i] = fields[i, at, :]


def outer_tile(from_left, from_right):
    return jnp.where(lanes(from_left.shape) % 8 >= 4, from_left, from_right)


def sides(near, far):
    right = odd_of("gz") == 0
    return jnp.where(right, far, near), jnp.where(right, near, far)


def corners(near, far, part, fields, first, second):
    del part
    odd = odd_of("gx") == 1
    for k, msg in enumerate((first, second)):
        low = odd if k == 0 else jnp.logical_not(odd)
        at = pl.ds(pl.multiple_of(jnp.where(low, 0, 56), 8), 8)
        keep = halves(low.astype(jnp.int32))
        tile = [outer_tile(*sides(near[t, at, :], far[t, at, :])) for t in range(3)]
        msg[0] = jnp.where(keep, tile[0], pltpu.roll(tile[1], 4, 0))
        msg[1] = jnp.where(keep, tile[2], 0.0)
        for i in range(2):
            msg[2 + i] = fields[36 + i, at, :]
        for n, (i, j) in enumerate(((38, 39), (40, 42), (41, 43))):
            msg[4 + n] = jnp.where(keep, fields[i, at, :], pltpu.roll(fields[j, at, :], 4, 0))


def spread(tile, j):
    x = jnp.where((lanes(tile.shape) // 8) % 4 == j, tile, 0.0)
    x = x + roll(x, -8 if j % 2 else 8)
    return x + roll(x, -16 if j >= 2 else 16)


def block_velocity(tile):
    x = spread(tile, 1)
    low, other = lanes(tile.shape) < 64, roll(x, 64)
    return jnp.where(low, x, other), jnp.where(low, other, x)


def block_kappa(kappa, t):
    block = lanes((1, 128)) // 8
    out = jnp.zeros((1, 128), F32)
    for j in range(4):
        for c in range(2):
            if 4 * t + j < 9:
                out = jnp.where((block % 4 == j) & (block // 8 == c), kappa[4 * t + j + 9 * c], out)
    return out


def block_sources(tiles, scale):
    shape = tiles[0].shape
    block = lanes(shape) // 8
    low, j = block < 8, block % 4
    ng = spread(tiles[2], 2)
    nucl, grow = jnp.where(low, ng, 0.0), jnp.where(low, roll(ng, 64), 0.0)
    y = spread(tiles[1], 2)
    birth = nucl * y * y
    sink = jnp.where(low, (0.3 * scale) * spread(tiles[0], 0), 0.0)
    before = (roll(tiles[0], 8), jnp.where(j == 0, roll(tiles[0], -24), roll(tiles[1], 8)))
    out = []
    for t in range(2):
        order = (scale / 3.0) * (j + 4 * t).astype(F32)
        out.append((0.5 * scale) * birth + (order * grow) * before[t] - sink * tiles[t])
    out[1] = jnp.where(j < 2, out[1], jnp.where(j == 2, (-0.2 * scale) * birth, 0.0))
    return out


def unpack(tile, b):
    lane = lanes(tile.shape)
    return jnp.where((lane < 4) | (lane >= 124), roll(tile, 124 - 8 * b), 0.0)


def sources(get, nucl, grow, scale):
    y = get(6)
    birth = nucl * y * y
    moms = [get(k) for k in range(6)]
    half = (0.5 * scale) * birth
    sink = (0.3 * scale) * moms[0]
    out = []
    for k in range(6):
        s = half - sink * moms[k]
        if k:
            s = s + ((scale * k / 3.0) * grow) * moms[k - 1]
        out.append(s)
    return out + [(-0.2 * scale) * birth]


def planes(p):
    for slot in range(4):
        field, ny = p + 9 * (slot // 2), slot % 2
        yield 2 * field + ny, field, ny, p // 4, 4 * slot + p % 4


def across(kq, g):
    return jnp.concatenate([*split(kq), *split(g)], axis=1)


def down_rows(kq, f):
    return jnp.concatenate([*split(kq), *split(f)], axis=0)


GROUP = 3


def groups(fn):
    def step(i, _):
        for k in range(GROUP):
            fn(i * GROUP + k)
        return _

    lax.fori_loop(0, 9 // GROUP, step, 0)


def plane_velocities(fields, us, ws, scale):
    for ny in range(2):
        us[ny] = fields[36 + ny] * (scale / first_part)
        ws[ny] = fields[38 + ny] * (scale / first_part)


def first_stage(kappa, fields, a_rows, z_main, part, us, ws):
    dt = time_step
    plane_velocities(fields, us, ws, dt)

    def one(p):
        lhs, rhs = [], []
        for i, field, ny, t, b in planes(p):
            v = fields[i]
            kq = (kappa[field] * (dt / second_part)) * v
            lhs.append(across(kq, ws[ny] * v))
            rhs.append(down_rows(kq, us[ny] * v))
        z = dot(jnp.concatenate(lhs, axis=0), z_main[...])
        x = [dot(a_rows[...], jnp.concatenate(rhs[c : c + 2], axis=1)) for c in (0, 2)]
        for n, (i, field, ny, t, b) in enumerate(planes(p)):
            part[i] = fields[i] + z[64 * n : 64 * n + 64] + x[n // 2][:, 128 * ny : 128 * ny + 128]

    groups(one)
    for ny in range(2):
        src = sources(lambda k: fields[2 * k + ny], fields[40 + ny], fields[42 + ny], dt)
        for k in range(7):
            part[2 * k + ny] += src[k]


def interior(
    kappa, fields, part, z_near, z_far, near, far, a_rows, z_main, z_outer, z_inner, q1, pq1, pws, half,
    us, ws, el, cor,
):
    dt, scale = time_step, 0.5 * time_step
    kap = [block_kappa(kappa, t) for t in range(3)]
    from_left, from_right, to_left, to_right = [], [], [], []
    for t in range(3):
        for pair, one, two in ((sides(near[t], far[t]), from_left, from_right), (sides(z_near[t], z_far[t]), to_left, to_right)):
            one.append(pair[0])
            two.append(pair[1])
    pus, rhs, outer = [], [], []
    for n, side in enumerate((from_left, to_left, from_right, to_right)):
        u, w = block_velocity(side[2])
        w = w * (dt / first_part)
        if n % 2 == 0:
            pus.append(u * (dt / first_part))
            rhs.append(w)
        for t in range(3):
            kq = (kap[t] * (dt / second_part)) * side[t]
            el[64 * t : 64 * t + 64, 512 * n : 512 * n + 512] = across(kq, w * side[t])
    z = dot(el[...], z_outer[...])
    u, w = outer_tile(*pus), outer_tile(*rhs)
    pws[...] = w
    outer = [outer_tile(from_left[t], from_right[t]) for t in range(3)]
    rhs = []
    for t in range(3):
        kq = (kap[t] * (dt / second_part)) * outer[t]
        el[64 * t : 64 * t + 64, 0:512] = across(kq, w * outer[t])
        rhs.append(down_rows(kq, u * outer[t]))
    cor[...] = dot(el[:, 0:512], z_inner[...])
    x = dot(a_rows[...], jnp.concatenate(rhs, axis=1))
    for t in range(3):
        pq1[t] = outer[t] + x[:, 128 * t : 128 * t + 128] + z[64 * t : 64 * t + 64]
    for t, src in enumerate(block_sources(outer, dt)):
        pq1[t] += src
    for p in range(9):
        for i, field, ny, t, b in planes(p):
            q1[i] = part[i] + unpack(cor[64 * t : 64 * t + 64, :], b)

    plane_velocities(fields, us, ws, scale)
    for t in range(3):
        e = pq1[t, 8:56, :]
        el[48 * t : 48 * t + 48, 0:512] = across((kap[t] * (scale / second_part)) * e, (0.5 * pws[8:56, :]) * e)
    cor[0:144, :] = dot(el[0:144, 0:512], z_inner[...])

    def two(p):
        lhs, rhs = [], []
        for i, field, ny, t, b in planes(p):
            v = q1[i]
            kq = (kappa[field] * (scale / second_part)) * v
            mid = v[8:56]
            lhs.append(across(kq[8:56], ws[ny, 8:56, :] * mid))
            rhs.append(down_rows(kq, us[ny] * v))
        z = dot(jnp.concatenate(lhs, axis=0), z_main[...])
        x = [dot(a_rows[8:56, :], jnp.concatenate(rhs[c : c + 2], axis=1)) for c in (0, 2)]
        for n, (i, field, ny, t, b) in enumerate(planes(p)):
            half[i, 8:56, :] = (
                0.5 * (fields[i, 8:56, :] + q1[i, 8:56, :])
                + z[48 * n : 48 * n + 48]
                + x[n // 2][:, 128 * ny : 128 * ny + 128]
                + unpack(cor[48 * t : 48 * t + 48, :], b)
            )

    for p in range(9):
        two(p)
    for ny in range(2):
        src = sources(
            lambda k: q1[2 * k + ny, 8:56, :], fields[40 + ny, 8:56, :], fields[42 + ny, 8:56, :], scale
        )
        for k in range(7):
            half[2 * k + ny, 8:56, :] += src[k]


def edges(
    kappa, fields, q1, pq1, pws, half, first, second, second_corner, first_corner,
    a_one, a_two, a_corner, z_main, z_inner, out_mom, out_sca,
    s1h, s1a, lz, done, sems,
):
    outs = [(out_mom, 0, 12), (out_sca, 12, 24)]
    copies = [
        pltpu.make_async_copy(
            half.at[pl.ds(at, size), pl.ds(8, 48)], out.at[pl.ds(0, size), pl.ds(8, 48)], sems.at[n]
        )
        for n, (out, at, size) in enumerate(outs)
    ]
    for copy in copies:
        copy.start()
    dt, scale = time_step, 0.5 * time_step
    one, two = dt / first_part, scale / first_part
    front = lax.broadcasted_iota(jnp.int32, (8, 128), 0) < 4
    below_first = halves(1 - odd_of("gx"))
    pair = lambda *tiles: jnp.concatenate(tiles, axis=0)
    at_h = lambda a, b, i: jnp.where(below_first, a[i], b[i])
    at_o = lambda a, b, i: jnp.where(below_first, b[i], a[i])
    at_a = lambda ref, *i: jnp.where(front, ref[*i, 0:8, :], ref[*i, 56:64, :])
    at_b = lambda ref, *i: jnp.where(front, ref[*i, 56:64, :], ref[*i, 0:8, :])
    at_c = lambda ref, *i: jnp.where(front, ref[*i, 8:16, :], ref[*i, 48:56, :])
    other_h = lambda a, b, i: pltpu.roll(at_o(a, b, i), 4, 0)

    uh = [at_h(first_corner, second_corner, 2 + ny) for ny in range(2)]
    uo = [at_o(first_corner, second_corner, 2 + ny) for ny in range(2)]
    wh = [at_h(first_corner, second_corner, 4) * one, other_h(first_corner, second_corner, 4) * one]
    ua = [at_a(fields, 36 + ny) for ny in range(2)]
    u_ho = [pair(uh[ny], uo[ny]) * one for ny in range(2)]
    u_hc = [pair(uh[ny], at_c(fields, 36 + ny)) * two for ny in range(2)]
    u_ab = [pair(ua[ny], at_b(fields, 36 + ny)) * two for ny in range(2)]
    w_ab = [pair(at_a(fields, 38 + ny), at_b(fields, 38 + ny)) * two for ny in range(2)]

    kap = [block_kappa(kappa, t) for t in range(3)]
    outer = [
        at_h(first_corner, second_corner, 0),
        other_h(first_corner, second_corner, 0),
        at_h(first_corner, second_corner, 1),
    ]
    u, w = block_velocity(outer[2])
    u, w = u * one, w * one
    rhs, kqs, gs = [], [], []
    for t in range(3):
        kq = (kap[t] * (dt / second_part)) * outer[t]
        rhs.append(pair(*split(pair(kq, u * outer[t]))))
        kqs.append(kq)
        gs.append(w * outer[t])
    zero = jnp.zeros((8, 128), F32)
    cor_h = dot(across(pair(*kqs, zero), pair(*gs, zero)), z_inner[...])
    x = dot(a_corner[...], jnp.concatenate(rhs, axis=1))
    lhs = []
    for t in range(3):
        e = pair(at_a(pq1, t) + x[0:8, 128 * t : 128 * t + 128], at_b(pq1, t))
        w = pair(at_a(pws), at_b(pws)) * 0.5
        lhs.append(across((kap[t] * (scale / second_part)) * e, w * e))
    cor_ab = dot(pair(*lhs), z_inner[...])

    hs = lambda i: at_h(first, second, i)
    for field in range(18):
        k = kappa[field] * (dt / second_part)
        h = [hs(2 * field + ny) for ny in range(2)]
        lz[16 * field : 16 * field + 16, :] = across(pair(k * h[0], k * h[1]), pair(wh[0] * h[0], wh[1] * h[1]))
    z = dot(lz[...], z_main[...])
    for p in range(9):
        rhs = []
        for i, field, ny, t, b in planes(p):
            k = kappa[field] * (dt / second_part)
            ho, a = pair(hs(i), at_o(first, second, i)), at_a(fields, i)
            rhs.append(down_rows(k * ho, u_ho[ny] * ho))
            rhs[-1] = pair(rhs[-1], *split(pair(k * a, (ua[ny] * one) * a)))
        x = dot(a_one[...], jnp.concatenate(rhs, axis=1))
        for n, (i, field, ny, t, b) in enumerate(planes(p)):
            at = 16 * field + 8 * ny
            x_i = x[:, 128 * n : 128 * n + 128]
            s1h[i] = hs(i) + x_i[0:8] + z[at : at + 8] + unpack(cor_h[8 * t : 8 * t + 8], b)
            s1a[i] = at_a(q1, i) + x_i[8:16]
    for ny in range(2):
        src = sources(
            lambda k: hs(2 * k + ny), at_h(first_corner, second_corner, 5 + ny), other_h(first_corner, second_corner, 5 + ny), dt
        )
        for k in range(7):
            s1h[2 * k + ny] += src[k]

    last = [
        pltpu.make_async_copy(
            done.at[pl.ds(at, size), pl.ds(8 * side, 8)],
            out.at[pl.ds(0, size), pl.ds(56 * side, 8)],
            sems.at[2 + 2 * n + side],
        )
        for n, (out, at, size) in enumerate(outs)
        for side in range(2)
    ]
    src = []
    for ny in range(2):
        nucl = pair(at_a(fields, 40 + ny), at_b(fields, 40 + ny))
        grow = pair(at_a(fields, 42 + ny), at_b(fields, 42 + ny))
        src.append(sources(lambda k: pair(s1a[2 * k + ny], at_b(q1, 2 * k + ny)), nucl, grow, scale))
    for p in range(9):
        if p == 6:
            for copy in last[:2]:
                copy.start()
        lhs, rhs = [], []
        for i, field, ny, t, b in planes(p):
            k = kappa[field] * (scale / second_part)
            ab, hc = pair(s1a[i], at_b(q1, i)), pair(s1h[i], at_c(q1, i))
            kq = split(k * ab)
            lhs.append(jnp.concatenate([*kq, *split(w_ab[ny] * ab)], axis=1))
            rhs.append(pair(*kq, *split(u_ab[ny] * ab), down_rows(k * hc, u_hc[ny] * hc)))
        z = dot(pair(*lhs), z_main[...])
        x = dot(a_two[...], jnp.concatenate(rhs, axis=1))
        for n, (i, field, ny, t, b) in enumerate(planes(p)):
            own = pair(at_a(fields, i) + s1a[i], at_b(fields, i) + at_b(q1, i))
            new = (
                0.5 * own
                + z[16 * n : 16 * n + 16]
                + x[:, 128 * n : 128 * n + 128]
                + unpack(cor_ab[16 * t : 16 * t + 16], b)
            )
            if field < 7:
                new = new + src[ny][field]
            done[i, 0:8, :] = jnp.where(front, new[0:8], new[8:16])
            done[i, 8:16, :] = jnp.where(front, new[8:16], new[0:8])
    for copy in last[2:]:
        copy.start()
    for copy in copies + last:
        copy.wait()


def call(kernel, outs, cost, mib=24, **kw):
    return pl.pallas_call(
        kernel,
        out_shape=[jax.ShapeDtypeStruct(o, F32) for o in outs],
        cost_estimate=pl.CostEstimate(flops=cost, bytes_accessed=cost // 4, transcendentals=0),
        compiler_params=pltpu.CompilerParams(vmem_limit_bytes=mib * 2**20),
        **kw,
    )


def swap(value, axis, far):
    peers = lax.axis_size(axis)
    other = lambda i: (((i + far) ^ 1) - far) % peers
    return lax.ppermute(value, axis, [(i, other(i)) for i in range(peers)])


def body(moments, scalars, velocity, diffusivity, nucleation, growth):
    vmem = pl.BlockSpec(memory_space=pltpu.VMEM)
    smem = pl.BlockSpec(memory_space=pltpu.SMEM)
    hbm = pl.BlockSpec(memory_space=pltpu.HBM)
    tiles = lambda *lead: pltpu.VMEM(lead + (128,), F32)
    flat = [
        pltpu.with_memory_space_constraint(x.reshape(-1, 64, 128), pltpu.HBM)
        for x in (moments, scalars, velocity, nucleation, growth)
    ]
    a_rows, a_one, a_two, a_corner, z_main, z_outer, z_inner = (jnp.asarray(m) for m in matrices())

    z_far, z_near, fields = call(
        pack_z,
        [(3, 64, 128), (3, 64, 128), (44, 64, 128)],
        10**6,
        in_specs=[hbm] * 5,
        out_specs=[vmem] * 3,
        scratch_shapes=[pltpu.SemaphoreType.DMA((10,))],
    )(*flat)
    far = swap(z_far, "gz", 1)
    x_first, x_second, z_near = call(x_messages, [(36, 8, 128), (36, 8, 128), (3, 64, 128)], 10**5)(fields, z_near)
    near = swap(z_near, "gz", 0)
    (part,) = call(
        first_stage,
        [(36, 64, 128)],
        10**7,
        in_specs=[smem] + [vmem] * 3,
        scratch_shapes=[tiles(2, 64), tiles(2, 64)],
    )(diffusivity, fields, a_rows, z_main)
    second = swap(x_second, "gx", 1)
    first = swap(x_first, "gx", 0)
    c_first, c_second = call(corners, [(7, 8, 128)] * 2, 10**6)(near, far, part, fields)
    second_corner = swap(c_second, "gx", 1)
    first_corner = swap(c_first, "gx", 0)
    q1, pq1, pws, half = call(
        interior,
        [(36, 64, 128), (3, 64, 128), (64, 128), (36, 64, 128)],
        10 * 10**8,
        in_specs=[smem] + [vmem] * 10,
        scratch_shapes=[tiles(2, 64), tiles(2, 64), pltpu.VMEM((192, 2048), BF16), tiles(192)],
    )(diffusivity, fields, part, z_near, z_far, near, far, a_rows, z_main, z_outer, z_inner)
    out_mom, out_sca = call(
        edges,
        [(12, 64, 128), (24, 64, 128)],
        10**8,
        in_specs=[smem] + [vmem] * 14,
        out_specs=[hbm] * 2,
        scratch_shapes=[
            tiles(36, 8), tiles(36, 8), pltpu.VMEM((288, 512), BF16), tiles(36, 16), pltpu.SemaphoreType.DMA((6,)),
        ],
    )(
        diffusivity, fields, q1, pq1, pws, half, first, second, second_corner, first_corner,
        a_one, a_two, a_corner, z_main, z_inner,
    )
    return out_mom.reshape(moments.shape), out_sca.reshape(scalars.shape)


def solution(mesh):
    return jax.shard_map(
        body,
        mesh=mesh,
        in_specs=(
            P(None, None, "gx", "gz"),
            P(None, None, "gx", "gz"),
            P(None, None, "gx", "gz"),
            P(),
            P(None, "gx", "gz"),
            P(None, "gx", "gz"),
        ),
        out_specs=(P(None, None, "gx", "gz"), P(None, None, "gx", "gz")),
        check_vma=False,
    )
```

```python
import numpy as np

import jax
import jax.numpy as jnp
from jax import lax
from jax.experimental import pallas as pl
from jax.experimental.pallas import tpu as pltpu
from jax.sharding import PartitionSpec as P

first_whole, first_part = (672.0, -168.0, 32.0, -3.0), 840.0
second_whole, second_part = (8064.0, -1008.0, 128.0, -9.0), 5040.0
centre_x, centre_z = -28672.0, -28.0
time_step = 0.25

F32, BF16 = jnp.float32, jnp.bfloat16


def band(targets, sources, centre):
    gap = np.asarray(sources)[None, :] - np.asarray(targets)[:, None]
    second = np.where(gap == 0, centre, 0.0)
    first = np.zeros(gap.shape)
    for m in range(1, 5):
        second = second + second_whole[m - 1] * (abs(gap) == m)
        first = first - first_whole[m - 1] * ((gap == m) * 1.0 - (gap == -m))
    return second, first


rows_h = [64, 65, 66, 67, -4, -3, -2, -1]
rows_o = [-8, -7, -6, -5, 68, 69, 70, 71]
rows_a = [0, 1, 2, 3, 60, 61, 62, 63]
rows_b = [56, 57, 58, 59, 4, 5, 6, 7]
rows_c = [8, 9, 10, 11, 52, 53, 54, 55]


def matrices():
    both = lambda pair, axis: np.concatenate([pair[0], pair[0], pair[1], pair[1]], axis=axis)
    rows, cols = np.arange(64), np.arange(128)
    a_rows = both(band(rows, rows, centre_x), 1)
    far = band(rows_h + rows_a, rows_h + rows_o, centre_x)
    own = [m * (np.arange(16) < 8)[:, None] for m in band(rows_h + rows_a, rows_a, centre_x)]
    a_one = np.concatenate([both(far, 1), own[0], own[1], own[0], own[1]], axis=1)
    a_two = np.concatenate(
        [both(band(rows_a + rows_b, src, centre_x), 1) for src in (rows_a + rows_b, rows_h + rows_c)], axis=1
    )
    corner = [np.concatenate([m, 0 * m]) for m in band(rows_a, rows_h, centre_x)]
    a_corner = np.concatenate(corner + corner, axis=1)
    z_main = both([m.T for m in band(cols, cols, centre_z)], 0)
    blocks = lambda pair: both([np.kron(np.eye(16), m.T) for m in pair], 0)
    outer = [128, 129, 130, 131, -4, -3, -2, -1]
    z_outer = np.concatenate(
        [blocks(band(outer, np.arange(at, at + 8), centre_z)) for at in (-8, 0, 128, 120)]
    )
    z_inner = blocks(band([124, 125, 126, 127, 0, 1, 2, 3], outer, centre_z))
    return [m.astype(BF16) for m in (a_rows, a_one, a_two, a_corner, z_main, z_outer, z_inner)]


def lanes(shape=(8, 128)):
    return lax.broadcasted_iota(jnp.int32, shape, len(shape) - 1)


def roll(x, by):
    by = by % 128
    return x if by == 0 else pltpu.roll(x, by, 1)


def split(x):
    high = x.astype(BF16)
    return high, (x - high.astype(F32)).astype(BF16)


def dot(a, b):
    return jnp.dot(a, b, preferred_element_type=F32)


def plane_of(p, s):
    c, ny = s // 2, s % 2
    return 2 * (p + 9 * c) + ny if p < 9 else 4 * p + s


def odd_of(axis):
    return lax.axis_index(axis) % 2


def z_tiles(fields, r, t):
    pair = lanes() // 16
    tile = [None, None]
    for j in range(4 if t < 2 else 3):
        for s in range(4):
            c = 2 * s + j // 2
            one = roll(fields[plane_of(4 * t + j, s), r : r + 8, :], 16 * c + 8)
            half = tile[j % 2]
            tile[j % 2] = one if half is None else jnp.where(pair == c, one, half)
    return tile


def pack_z(mom, sca, vel, nuc, gro, far, near, fields, sems):
    parts = [
        [(mom, 0, 0, 8), (sca, 6, 18, 8)],
        [(mom, 8, 8, 4), (sca, 0, 12, 4), (sca, 14, 26, 8)],
        [(sca, 4, 16, 2), (sca, 22, 34, 2), (vel, 0, 36, 4), (nuc, 0, 40, 2), (gro, 0, 42, 2)],
    ]
    copies, n = [], 0
    for part in parts:
        copies.append([])
        for src, at, to, size in part:
            copies[-1].append(
                pltpu.make_async_copy(src.at[pl.ds(at, size)], fields.at[pl.ds(to, size)], sems.at[n])
            )
            copies[-1][-1].start()
            n += 1
    right = odd_of("gz") == 0
    odd = (lanes() // 8) % 2 == 1
    for t in range(3):
        for copy in copies[t]:
            copy.wait()
        made = [z_tiles(fields, r, t) for r in range(0, 64, 8)]
        for n, (one, two) in enumerate(made):
            zl, zr = jnp.where(odd, two, roll(one, -8)), jnp.where(odd, roll(two, 8), one)
            far[t, 8 * n : 8 * n + 8, :] = jnp.where(right, zl, zr)
            near[t, 8 * n : 8 * n + 8, :] = jnp.where(right, zr, zl)


def halves(first):
    return (lax.broadcasted_iota(jnp.int32, (8, 128), 0) + 4 * first) % 8 >= 4


def x_messages(fields, first, second):
    odd = odd_of("gx") == 1
    for k, msg in enumerate((first, second)):
        low = odd if k == 0 else jnp.logical_not(odd)
        at = pl.ds(pl.multiple_of(jnp.where(low, 0, 56), 8), 8)
        for i in range(36):
            msg[i] = fields[i, at, :]


def outer_tile(from_left, from_right):
    return jnp.where(lanes(from_left.shape) % 8 >= 4, from_left, from_right)


def sides(near, far):
    right = odd_of("gz") == 0
    return jnp.where(right, far, near), jnp.where(right, near, far)


def corners(near, far, part, fields, first, second):
    del part
    odd = odd_of("gx") == 1
    for k, msg in enumerate((first, second)):
        low = odd if k == 0 else jnp.logical_not(odd)
        at = pl.ds(pl.multiple_of(jnp.where(low, 0, 56), 8), 8)
        keep = halves(low.astype(jnp.int32))
        tile = [outer_tile(*sides(near[t, at, :], far[t, at, :])) for t in range(3)]
        msg[0] = jnp.where(keep, tile[0], pltpu.roll(tile[1], 4, 0))
        msg[1] = jnp.where(keep, tile[2], 0.0)
        for i in range(2):
            msg[2 + i] = fields[36 + i, at, :]
        for n, (i, j) in enumerate(((38, 39), (40, 42), (41, 43))):
            msg[4 + n] = jnp.where(keep, fields[i, at, :], pltpu.roll(fields[j, at, :], 4, 0))


def spread(tile, j):
    x = jnp.where((lanes(tile.shape) // 8) % 4 == j, tile, 0.0)
    x = x + roll(x, -8 if j % 2 else 8)
    return x + roll(x, -16 if j >= 2 else 16)


def block_velocity(tile):
    x = spread(tile, 1)
    low, other = lanes(tile.shape) < 64, roll(x, 64)
    return jnp.where(low, x, other), jnp.where(low, other, x)


def block_kappa(kappa, t):
    block = lanes((1, 128)) // 8
    out = jnp.zeros((1, 128), F32)
    for j in range(4):
        for c in range(2):
            if 4 * t + j < 9:
                out = jnp.where((block % 4 == j) & (block // 8 == c), kappa[4 * t + j + 9 * c], out)
    return out


def block_sources(tiles, scale):
    shape = tiles[0].shape
    block = lanes(shape) // 8
    low, j = block < 8, block % 4
    ng = spread(tiles[2], 2)
    nucl, grow = jnp.where(low, ng, 0.0), jnp.where(low, roll(ng, 64), 0.0)
    y = spread(tiles[1], 2)
    birth = nucl * y * y
    sink = jnp.where(low, (0.3 * scale) * spread(tiles[0], 0), 0.0)
    before = (roll(tiles[0], 8), jnp.where(j == 0, roll(tiles[0], -24), roll(tiles[1], 8)))
    out = []
    for t in range(2):
        order = (scale / 3.0) * (j + 4 * t).astype(F32)
        out.append((0.5 * scale) * birth + (order * grow) * before[t] - sink * tiles[t])
    out[1] = jnp.where(j < 2, out[1], jnp.where(j == 2, (-0.2 * scale) * birth, 0.0))
    return out


def unpack(tile, b):
    lane = lanes(tile.shape)
    return jnp.where((lane < 4) | (lane >= 124), roll(tile, 124 - 8 * b), 0.0)


def sources(get, nucl, grow, scale):
    y = get(6)
    birth = nucl * y * y
    moms = [get(k) for k in range(6)]
    half = (0.5 * scale) * birth
    sink = (0.3 * scale) * moms[0]
    out = []
    for k in range(6):
        s = half - sink * moms[k]
        if k:
            s = s + ((scale * k / 3.0) * grow) * moms[k - 1]
        out.append(s)
    return out + [(-0.2 * scale) * birth]


def planes(p):
    for slot in range(4):
        field, ny = p + 9 * (slot // 2), slot % 2
        yield 2 * field + ny, field, ny, p // 4, 4 * slot + p % 4


def across(kq, g):
    return jnp.concatenate([*split(kq), *split(g)], axis=1)


def down_rows(kq, f):
    return jnp.concatenate([*split(kq), *split(f)], axis=0)


GROUP = 3


def groups(fn):
    def step(i, _):
        for k in range(GROUP):
            fn(i * GROUP + k)
        return _

    lax.fori_loop(0, 9 // GROUP, step, 0)


def plane_velocities(fields, us, ws, scale):
    for ny in range(2):
        us[ny] = fields[36 + ny] * (scale / first_part)
        ws[ny] = fields[38 + ny] * (scale / first_part)


def first_stage(kappa, fields, a_rows, z_main, part, us, ws):
    dt = time_step
    plane_velocities(fields, us, ws, dt)

    def one(p):
        lhs, rhs = [], []
        for i, field, ny, t, b in planes(p):
            v = fields[i]
            kq = (kappa[field] * (dt / second_part)) * v
            lhs.append(across(kq, ws[ny] * v))
            rhs.append(down_rows(kq, us[ny] * v))
        z = dot(jnp.concatenate(lhs, axis=0), z_main[...])
        x = [dot(a_rows[...], jnp.concatenate(rhs[c : c + 2], axis=1)) for c in (0, 2)]
        for n, (i, field, ny, t, b) in enumerate(planes(p)):
            part[i] = fields[i] + z[64 * n : 64 * n + 64] + x[n // 2][:, 128 * ny : 128 * ny + 128]

    groups(one)
    for ny in range(2):
        src = sources(lambda k: fields[2 * k + ny], fields[40 + ny], fields[42 + ny], dt)
        for k in range(7):
            part[2 * k + ny] += src[k]


def interior(
    kappa, fields, part, z_near, z_far, near, far, a_rows, z_main, z_outer, z_inner, q1, pq1, pws, half,
    us, ws, el, cor, cor_two,
):
    dt, scale = time_step, 0.5 * time_step
    kap = [block_kappa(kappa, t) for t in range(3)]
    from_left, from_right, to_left, to_right = [], [], [], []
    for t in range(3):
        for pair, one, two in ((sides(near[t], far[t]), from_left, from_right), (sides(z_near[t], z_far[t]), to_left, to_right)):
            one.append(pair[0])
            two.append(pair[1])
    pus, rhs, outer = [], [], []
    for n, side in enumerate((from_left, to_left, from_right, to_right)):
        u, w = block_velocity(side[2])
        w = w * (dt / first_part)
        if n % 2 == 0:
            pus.append(u * (dt / first_part))
            rhs.append(w)
        for t in range(3):
            kq = (kap[t] * (dt / second_part)) * side[t]
            el[64 * t : 64 * t + 64, 512 * n : 512 * n + 512] = across(kq, w * side[t])
    z = dot(el[...], z_outer[...])
    u, w = outer_tile(*pus), outer_tile(*rhs)
    pws[...] = w
    outer = [outer_tile(from_left[t], from_right[t]) for t in range(3)]
    rhs = []
    for t in range(3):
        kq = (kap[t] * (dt / second_part)) * outer[t]
        el[64 * t : 64 * t + 64, 0:512] = across(kq, w * outer[t])
        rhs.append(down_rows(kq, u * outer[t]))
    cor[...] = dot(el[:, 0:512], z_inner[...])
    x = dot(a_rows[...], jnp.concatenate(rhs, axis=1))
    for t in range(3):
        pq1[t] = outer[t] + x[:, 128 * t : 128 * t + 128] + z[64 * t : 64 * t + 64]
    for t, src in enumerate(block_sources(outer, dt)):
        pq1[t] += src
    plane_velocities(fields, us, ws, scale)
    for t in range(3):
        e = pq1[t, 8:56, :]
        el[48 * t : 48 * t + 48, 0:512] = across((kap[t] * (scale / second_part)) * e, (0.5 * pws[8:56, :]) * e)
    cor_two[...] = dot(el[0:144, 0:512], z_inner[...])

    def two(p):
        lhs, rhs = [], []
        for i, field, ny, t, b in planes(p):
            v = part[i] + unpack(cor[64 * t : 64 * t + 64, :], b)
            q1[i] = v
            kq = (kappa[field] * (scale / second_part)) * v
            mid = v[8:56]
            lhs.append(across(kq[8:56], ws[ny, 8:56, :] * mid))
            rhs.append(down_rows(kq, us[ny] * v))
        z = dot(jnp.concatenate(lhs, axis=0), z_main[...])
        x = [dot(a_rows[8:56, :], jnp.concatenate(rhs[c : c + 2], axis=1)) for c in (0, 2)]
        for n, (i, field, ny, t, b) in enumerate(planes(p)):
            half[i, 8:56, :] = (
                0.5 * (fields[i, 8:56, :] + q1[i, 8:56, :])
                + z[48 * n : 48 * n + 48]
                + x[n // 2][:, 128 * ny : 128 * ny + 128]
                + unpack(cor_two[48 * t : 48 * t + 48, :], b)
            )

    for p in range(9):
        two(p)
    for ny in range(2):
        src = sources(
            lambda k: q1[2 * k + ny, 8:56, :], fields[40 + ny, 8:56, :], fields[42 + ny, 8:56, :], scale
        )
        for k in range(7):
            half[2 * k + ny, 8:56, :] += src[k]


def edges(
    kappa, fields, q1, pq1, pws, half, first, second, second_corner, first_corner,
    a_one, a_two, a_corner, z_main, z_inner, out_mom, out_sca,
    s1h, s1a, lz, done, sems,
):
    outs = [(out_mom, 0, 12), (out_sca, 12, 24)]
    copies = [
        pltpu.make_async_copy(
            half.at[pl.ds(at, size), pl.ds(8, 48)], out.at[pl.ds(0, size), pl.ds(8, 48)], sems.at[n]
        )
        for n, (out, at, size) in enumerate(outs)
    ]
    for copy in copies:
        copy.start()
    dt, scale = time_step, 0.5 * time_step
    one, two = dt / first_part, scale / first_part
    front = lax.broadcasted_iota(jnp.int32, (8, 128), 0) < 4
    below_first = halves(1 - odd_of("gx"))
    pair = lambda *tiles: jnp.concatenate(tiles, axis=0)
    at_h = lambda a, b, i: jnp.where(below_first, a[i], b[i])
    at_o = lambda a, b, i: jnp.where(below_first, b[i], a[i])
    at_a = lambda ref, *i: jnp.where(front, ref[*i, 0:8, :], ref[*i, 56:64, :])
    at_b = lambda ref, *i: jnp.where(front, ref[*i, 56:64, :], ref[*i, 0:8, :])
    at_c = lambda ref, *i: jnp.where(front, ref[*i, 8:16, :], ref[*i, 48:56, :])
    other_h = lambda a, b, i: pltpu.roll(at_o(a, b, i), 4, 0)

    uh = [at_h(first_corner, second_corner, 2 + ny) for ny in range(2)]
    uo = [at_o(first_corner, second_corner, 2 + ny) for ny in range(2)]
    wh = [at_h(first_corner, second_corner, 4) * one, other_h(first_corner, second_corner, 4) * one]
    ua = [at_a(fields, 36 + ny) for ny in range(2)]
    u_ho = [pair(uh[ny], uo[ny]) * one for ny in range(2)]
    u_hc = [pair(uh[ny], at_c(fields, 36 + ny)) * two for ny in range(2)]
    u_ab = [pair(ua[ny], at_b(fields, 36 + ny)) * two for ny in range(2)]
    w_ab = [pair(at_a(fields, 38 + ny), at_b(fields, 38 + ny)) * two for ny in range(2)]

    kap = [block_kappa(kappa, t) for t in range(3)]
    outer = [
        at_h(first_corner, second_corner, 0),
        other_h(first_corner, second_corner, 0),
        at_h(first_corner, second_corner, 1),
    ]
    u, w = block_velocity(outer[2])
    u, w = u * one, w * one
    rhs, kqs, gs = [], [], []
    for t in range(3):
        kq = (kap[t] * (dt / second_part)) * outer[t]
        rhs.append(pair(*split(pair(kq, u * outer[t]))))
        kqs.append(kq)
        gs.append(w * outer[t])
    zero = jnp.zeros((8, 128), F32)
    cor_h = dot(across(pair(*kqs, zero), pair(*gs, zero)), z_inner[...])
    x = dot(a_corner[...], jnp.concatenate(rhs, axis=1))
    lhs = []
    for t in range(3):
        e = pair(at_a(pq1, t) + x[0:8, 128 * t : 128 * t + 128], at_b(pq1, t))
        w = pair(at_a(pws), at_b(pws)) * 0.5
        lhs.append(across((kap[t] * (scale / second_part)) * e, w * e))
    cor_ab = dot(pair(*lhs), z_inner[...])

    hs = lambda i: at_h(first, second, i)
    for field in range(18):
        k = kappa[field] * (dt / second_part)
        h = [hs(2 * field + ny) for ny in range(2)]
        lz[16 * field : 16 * field + 16, :] = across(pair(k * h[0], k * h[1]), pair(wh[0] * h[0], wh[1] * h[1]))
    z = dot(lz[...], z_main[...])
    for p in range(9):
        rhs = []
        for i, field, ny, t, b in planes(p):
            k = kappa[field] * (dt / second_part)
            ho, a = pair(hs(i), at_o(first, second, i)), at_a(fields, i)
            rhs.append(down_rows(k * ho, u_ho[ny] * ho))
            rhs[-1] = pair(rhs[-1], *split(pair(k * a, (ua[ny] * one) * a)))
        x = dot(a_one[...], jnp.concatenate(rhs, axis=1))
        for n, (i, field, ny, t, b) in enumerate(planes(p)):
            at = 16 * field + 8 * ny
            x_i = x[:, 128 * n : 128 * n + 128]
            s1h[i] = hs(i) + x_i[0:8] + z[at : at + 8] + unpack(cor_h[8 * t : 8 * t + 8], b)
            s1a[i] = at_a(q1, i) + x_i[8:16]
    for ny in range(2):
        src = sources(
            lambda k: hs(2 * k + ny), at_h(first_corner, second_corner, 5 + ny), other_h(first_corner, second_corner, 5 + ny), dt
        )
        for k in range(7):
            s1h[2 * k + ny] += src[k]

    last = [
        pltpu.make_async_copy(
            done.at[pl.ds(at, size), pl.ds(8 * side, 8)],
            out.at[pl.ds(0, size), pl.ds(56 * side, 8)],
            sems.at[2 + 2 * n + side],
        )
        for n, (out, at, size) in enumerate(outs)
        for side in range(2)
    ]
    src = []
    for ny in range(2):
        nucl = pair(at_a(fields, 40 + ny), at_b(fields, 40 + ny))
        grow = pair(at_a(fields, 42 + ny), at_b(fields, 42 + ny))
        src.append(sources(lambda k: pair(s1a[2 * k + ny], at_b(q1, 2 * k + ny)), nucl, grow, scale))
    for p in range(9):
        if p == 6:
            for copy in last[:2]:
                copy.start()
        lhs, rhs = [], []
        for i, field, ny, t, b in planes(p):
            k = kappa[field] * (scale / second_part)
            ab, hc = pair(s1a[i], at_b(q1, i)), pair(s1h[i], at_c(q1, i))
            kq = split(k * ab)
            lhs.append(jnp.concatenate([*kq, *split(w_ab[ny] * ab)], axis=1))
            rhs.append(pair(*kq, *split(u_ab[ny] * ab), down_rows(k * hc, u_hc[ny] * hc)))
        z = dot(pair(*lhs), z_main[...])
        x = dot(a_two[...], jnp.concatenate(rhs, axis=1))
        for n, (i, field, ny, t, b) in enumerate(planes(p)):
            own = pair(at_a(fields, i) + s1a[i], at_b(fields, i) + at_b(q1, i))
            new = (
                0.5 * own
                + z[16 * n : 16 * n + 16]
                + x[:, 128 * n : 128 * n + 128]
                + unpack(cor_ab[16 * t : 16 * t + 16], b)
            )
            if field < 7:
                new = new + src[ny][field]
            done[i, 0:8, :] = jnp.where(front, new[0:8], new[8:16])
            done[i, 8:16, :] = jnp.where(front, new[8:16], new[0:8])
    for copy in last[2:]:
        copy.start()
    for copy in copies + last:
        copy.wait()


def call(kernel, outs, cost, mib=24, **kw):
    return pl.pallas_call(
        kernel,
        out_shape=[jax.ShapeDtypeStruct(o, F32) for o in outs],
        cost_estimate=pl.CostEstimate(flops=cost, bytes_accessed=cost // 4, transcendentals=0),
        compiler_params=pltpu.CompilerParams(vmem_limit_bytes=mib * 2**20),
        **kw,
    )


def swap(value, axis, far):
    peers = lax.axis_size(axis)
    other = lambda i: (((i + far) ^ 1) - far) % peers
    return lax.ppermute(value, axis, [(i, other(i)) for i in range(peers)])


def body(moments, scalars, velocity, diffusivity, nucleation, growth):
    vmem = pl.BlockSpec(memory_space=pltpu.VMEM)
    smem = pl.BlockSpec(memory_space=pltpu.SMEM)
    hbm = pl.BlockSpec(memory_space=pltpu.HBM)
    tiles = lambda *lead: pltpu.VMEM(lead + (128,), F32)
    flat = [
        pltpu.with_memory_space_constraint(x.reshape(-1, 64, 128), pltpu.HBM)
        for x in (moments, scalars, velocity, nucleation, growth)
    ]
    a_rows, a_one, a_two, a_corner, z_main, z_outer, z_inner = (jnp.asarray(m) for m in matrices())

    z_far, z_near, fields = call(
        pack_z,
        [(3, 64, 128), (3, 64, 128), (44, 64, 128)],
        10**6,
        in_specs=[hbm] * 5,
        out_specs=[vmem] * 3,
        scratch_shapes=[pltpu.SemaphoreType.DMA((10,))],
    )(*flat)
    far = swap(z_far, "gz", 1)
    x_first, x_second = call(x_messages, [(36, 8, 128), (36, 8, 128)], 10**5)(fields)
    near = swap(z_near, "gz", 0)
    (part,) = call(
        first_stage,
        [(36, 64, 128)],
        10**7,
        in_specs=[smem] + [vmem] * 3,
        scratch_shapes=[tiles(2, 64), tiles(2, 64)],
    )(diffusivity, fields, a_rows, z_main)
    second = swap(x_second, "gx", 1)
    first = swap(x_first, "gx", 0)
    c_first, c_second = call(corners, [(7, 8, 128)] * 2, 10**6)(near, far, part, fields)
    second_corner = swap(c_second, "gx", 1)
    first_corner = swap(c_first, "gx", 0)
    q1, pq1, pws, half = call(
        interior,
        [(36, 64, 128), (3, 64, 128), (64, 128), (36, 64, 128)],
        10 * 10**8,
        in_specs=[smem] + [vmem] * 10,
        scratch_shapes=[tiles(2, 64), tiles(2, 64), pltpu.VMEM((192, 2048), BF16), tiles(192), tiles(144)],
    )(diffusivity, fields, part, z_near, z_far, near, far, a_rows, z_main, z_outer, z_inner)
    out_mom, out_sca = call(
        edges,
        [(12, 64, 128), (24, 64, 128)],
        10**8,
        in_specs=[smem] + [vmem] * 14,
        out_specs=[hbm] * 2,
        scratch_shapes=[
            tiles(36, 8), tiles(36, 8), pltpu.VMEM((288, 512), BF16), tiles(36, 16), pltpu.SemaphoreType.DMA((6,)),
        ],
    )(
        diffusivity, fields, q1, pq1, pws, half, first, second, second_corner, first_corner,
        a_one, a_two, a_corner, z_main, z_inner,
    )
    return out_mom.reshape(moments.shape), out_sca.reshape(scalars.shape)


def solution(mesh):
    return jax.shard_map(
        body,
        mesh=mesh,
        in_specs=(
            P(None, None, "gx", "gz"),
            P(None, None, "gx", "gz"),
            P(None, None, "gx", "gz"),
            P(),
            P(None, "gx", "gz"),
            P(None, "gx", "gz"),
        ),
        out_specs=(P(None, None, "gx", "gz"), P(None, None, "gx", "gz")),
        check_vma=False,
    )
```
